32 devices in a mesh: dp: 4 (over z), head: 2 (over x), srv: 4 (over y, core).
Axes of the slice: x: 2, y: 2, z: 4, core: 2. Of those that a mesh axis runs over, the one named last changes fastest.
Arguments:
- queries: bfloat16 [512, 8, 1024], P('dp', 'srv', 'head'), may hold values from -5 to 5
- keys: bfloat16 [2560, 1024], P(('dp', 'head')), may hold values from -5 to 5
- values: bfloat16 [2560, 1024], P(('dp', 'head')), may hold values from -6 to 6
- output_gradient: bfloat16 [512, 8, 1024], P('dp', 'srv', 'head'), may hold values from -6 to 6
- doc_ids: int32 [2560], P('dp'), may hold values from 0 to 7, never falling along the last dimension, each value on 1 to 1280 neighbouring positions
Outputs:
- attention: bfloat16 [512, 8, 1024], P('dp', 'srv', 'head')
- q_grad: bfloat16 [512, 8, 1024], P('dp', 'srv', 'head')
- k_grad: bfloat16 [2560, 1024], P(('dp', 'head', 'srv'))
- v_grad: bfloat16 [2560, 1024], P(('dp', 'head', 'srv'))
The draws below stay inside these ranges and needn't reach their ends.
Inputs may be any that keep to these rules, and one draw needn't show every extreme that they name: `doc_ids`: document numbers never fall along the keys; every document holds at most 1280 keys, and one holds exactly 1280.
All inputs are finite; a program needn't handle non-finite values.
Results may differ from the reference program's by a relative error of at most 0.039.
Values may be sent and summed in bfloat16 or wider, within the bound.
A program may use at most 64 MiB of HBM per device.

```python
import math
import jax
import jax.numpy as jnp
import numpy as np
from jax import lax

HEAD_SIZE = 128
KEY_VALUE_HEADS = 8
QUERY_PER_KV = 8
DOCS = 8
QUERY_ROWS = 512
CONTEXT_KEYS = 2048
KEYS_PER_SHARD = 640
KEY_TOTAL = 2560
DOC_MAX = 1280
N_DP = 4


def draw_queries(key, part):
    local_key_rows = jax.random.fold_in(key, 101)
    final_output = jnp.clip(jax.random.normal(local_key_rows, (QUERY_ROWS, QUERY_PER_KV, KEY_VALUE_HEADS * HEAD_SIZE), jnp.float32), -5.0, 5.0)
    return final_output.astype(jnp.bfloat16)


def draw_keys(key, part):
    local_key_rows = jax.random.fold_in(key, 202)
    final_output = jnp.clip(jax.random.normal(local_key_rows, (KEY_TOTAL, KEY_VALUE_HEADS * HEAD_SIZE), jnp.float32), -5.0, 5.0)
    return final_output.astype(jnp.bfloat16)


def shard_levels(stream_key, extent, pieces, least, high):
    gain = 1.0
    for dim, blocks in pieces:
        draws = jax.random.uniform(jax.random.fold_in(jax.random.fold_in(stream_key, 6), dim), (blocks,), jnp.float32, least / len(pieces), high / len(pieces))
        gain = gain * jnp.repeat(jnp.exp(draws), extent[dim] // blocks).reshape((-1,) + (1,) * (len(extent) - 1 - dim))
    return gain


def profile(amount, total, limit, slope):
    weights = [(1 << 20) // math.isqrt(standing ** slope) + 1 for standing in range(2, amount + 1)]
    surplus, holding = total - limit - (amount - 1), [1] * (amount - 1)
    while surplus > 0:
        free = [i for i in range(amount - 1) if holding[i] < limit]
        whole, budget = sum([weights[i] for i in free]), surplus
        for i in free:
            more = min(limit - holding[i], max(1, budget * weights[i] // whole), surplus)
            holding[i] = holding[i] + more
            surplus = surplus - more
    return np.array([limit] + holding)


def ragged_sizes(rng, amount, total, most, slope):
    if amount == 2:
        one = jax.random.randint(rng, (), max(1, total - most), min(most, total - 1) + 1)
        return jnp.stack([one, total - one])
    tallies = jnp.asarray(profile(amount, total, most, slope), jnp.int32)
    pairs = (amount - 1) // 2
    giver, sink = tallies[1:1 + 2 * pairs:2], tallies[2:2 + 2 * pairs:2]
    room = jnp.minimum(giver - 1, most - sink)
    shifted = jax.random.randint(jax.random.fold_in(rng, 1), (pairs,), 0, 1 << 20) % (room + 1)
    tallies = tallies.at[1:1 + 2 * pairs:2].set(giver - shifted).at[2:2 + 2 * pairs:2].set(sink + shifted)
    return tallies[jax.random.permutation(jax.random.fold_in(rng, 2), amount)]


def gaussian(rng, dims, scale, reach, shards=(), kind=jnp.bfloat16):
    loudness = shard_levels(rng, dims, shards, -0.22, 0.18) if shards else 1.0
    values = jax.random.normal(rng, dims, jnp.float32) * scale * loudness
    return jnp.minimum(jnp.maximum(values, -reach), reach).astype(kind)


def setup_inputs(seed: int = 0) -> dict:
    key_of = jax.random.split(jax.random.key(seed), 6)
    return {
        "queries": draw_queries(jax.random.fold_in(key_of[5], 71), 0),
        "keys": draw_keys(jax.random.fold_in(key_of[5], 71), 0),
        "values": gaussian(key_of[2], (KEY_TOTAL, KEY_VALUE_HEADS * HEAD_SIZE), 1.0, 6.0, ((0, 8),)),
        "output_gradient": gaussian(key_of[3], (QUERY_ROWS, QUERY_PER_KV, KEY_VALUE_HEADS * HEAD_SIZE), 1.0, 6.0, ((0, 4), (1, 4), (2, 2))),
        "doc_ids": jnp.searchsorted(jnp.cumsum(ragged_sizes(key_of[4], DOCS, KEY_TOTAL, DOC_MAX, 2)), jnp.arange(KEY_TOTAL), side="right").astype(jnp.int32),
    }


NEGATIVE = -1.0e30


def settle(array_f32):
    rounded = lax.optimization_barrier(array_f32.astype(jnp.bfloat16))
    return rounded.astype(jnp.float32)


def reference(queries, keys, values, output_gradient, doc_ids):
    scale_factor = HEAD_SIZE ** -0.5
    query_head_rows = queries.astype(jnp.float32).reshape(QUERY_ROWS, QUERY_PER_KV, KEY_VALUE_HEADS, HEAD_SIZE)
    gradient_per_head = output_gradient.astype(jnp.float32).reshape(QUERY_ROWS, QUERY_PER_KV, KEY_VALUE_HEADS, HEAD_SIZE)
    key_tiles = keys.astype(jnp.float32).reshape(N_DP, KEYS_PER_SHARD, KEY_VALUE_HEADS, HEAD_SIZE)
    value_tiles = values.astype(jnp.float32).reshape(N_DP, KEYS_PER_SHARD, KEY_VALUE_HEADS, HEAD_SIZE)
    query_at = CONTEXT_KEYS + jnp.arange(QUERY_ROWS, dtype=jnp.int32)
    query_doc = doc_ids[CONTEXT_KEYS:]
    key_at = jnp.arange(KEY_TOTAL, dtype=jnp.int32).reshape(N_DP, KEYS_PER_SHARD)
    key_doc = doc_ids.reshape(N_DP, KEYS_PER_SHARD)
    indices = jnp.arange(N_DP, dtype=jnp.int32)

    def allowed_of(index):
        earlier = key_at[index][None, :] <= query_at[:, None]
        same_doc = key_doc[index][None, :] == query_doc[:, None]
        return (earlier & same_doc)[None, None]

    def scores_of(index):
        return jnp.einsum("qjgd,kgd->gjqk", query_head_rows, key_tiles[index]) * scale_factor

    def block_max(index):
        return jnp.max(jnp.where(allowed_of(index), scores_of(index), NEGATIVE), axis=-1)

    row_max = jnp.max(lax.map(block_max, indices), axis=0)

    def forward_step(totals, index):
        weights = jnp.where(allowed_of(index), jnp.exp(scores_of(index) - row_max[..., None]), 0.0)
        weighted = jnp.einsum("gjqk,kgd->gjqd", settle(weights), value_tiles[index])
        return (totals[0] + weighted, totals[1] + jnp.sum(weights, axis=-1)), index

    empty_output = jnp.zeros((KEY_VALUE_HEADS, QUERY_PER_KV, QUERY_ROWS, HEAD_SIZE), jnp.float32)
    empty_norm = jnp.zeros((KEY_VALUE_HEADS, QUERY_PER_KV, QUERY_ROWS), jnp.float32)
    (summed, norm_sum), unused = lax.scan(forward_step, (empty_output, empty_norm), indices)
    attention = (summed / norm_sum[..., None]).transpose(2, 1, 0, 3).astype(jnp.bfloat16)
    log_norm = row_max + jnp.log(norm_sum)
    row_delta = jnp.sum(gradient_per_head * attention.astype(jnp.float32), axis=-1).transpose(2, 1, 0)

    def backward_step(query_row_count, index):
        probs = jnp.where(allowed_of(index), jnp.exp(scores_of(index) - log_norm[..., None]), 0.0)
        value_grad = jnp.einsum("gjqk,qjgd->kgd", settle(probs), gradient_per_head)
        weight_grad = jnp.einsum("qjgd,kgd->gjqk", gradient_per_head, value_tiles[index])
        score_grad = settle(probs * (weight_grad - row_delta[..., None]))
        q_term = jnp.einsum("gjqk,kgd->qjgd", score_grad, key_tiles[index]) * scale_factor
        key_grad = jnp.einsum("gjqk,qjgd->kgd", score_grad, query_head_rows) * scale_factor
        return query_row_count + settle(q_term), (key_grad, value_grad)

    query_offset = jnp.zeros((QUERY_ROWS, QUERY_PER_KV, KEY_VALUE_HEADS, HEAD_SIZE), jnp.float32)
    query_row_count, (key_gradient_rows, value_gradient_rows) = lax.scan(backward_step, query_offset, indices)
    return (attention.reshape(QUERY_ROWS, QUERY_PER_KV, KEY_VALUE_HEADS * HEAD_SIZE),
            query_row_count.reshape(QUERY_ROWS, QUERY_PER_KV, KEY_VALUE_HEADS * HEAD_SIZE).astype(jnp.bfloat16),
            key_gradient_rows.reshape(KEY_TOTAL, KEY_VALUE_HEADS * HEAD_SIZE).astype(jnp.bfloat16),
            value_gradient_rows.reshape(KEY_TOTAL, KEY_VALUE_HEADS * HEAD_SIZE).astype(jnp.bfloat16))
```

```python
import functools
import math

import jax
import jax.numpy as jnp
from jax import lax
from jax.experimental import pallas as pl
from jax.experimental.pallas import tpu as pltpu
from jax.sharding import PartitionSpec as P

HEAD_SIZE = 128


NEGATIVE = -1e30
MESH = pl.DeviceIdType.MESH
AXES = ("dp", "head", "srv")


def attend(sizes, qd_ref, k_ref, v_ref, doc_ref, att_ref, dq_ref, kg_ref, vg_ref,
           qd_buf, kv_buf, kt_buf, vt_buf, docs, bias, acc, grad_out, att_out, dq_out, grad_in, total,
           q_sem, q_got, kv_sem, kv_got, doc_sem, doc_got, att_sem, att_got, dq_sem, dq_got, g_sem, g_got):
    dp, heads, srv, home, pair, rows, first, window = sizes
    chunk = math.gcd(home, rows)
    chunks = rows // chunk
    piece = rows // srv
    wide = pair * home
    pad = piece
    scale = HEAD_SIZE ** (-0.5)
    z, x, v = (lax.axis_index(name) for name in AXES)
    place = z * heads + x
    base = place * rows
    low = first + home * z
    device_count = dp * heads * srv
    me = place * srv + v

    def device(index):
        return (index // (heads * srv), (index // srv) % heads, index % srv)

    def send(here, src, dst, send_sem, recv_sem, target):
        @pl.when(here)
        def _():
            pltpu.make_async_copy(src, dst, recv_sem).start()

        @pl.when(jnp.logical_not(here))
        def _():
            pltpu.make_async_remote_copy(
                src_ref=src, dst_ref=dst, send_sem=send_sem, recv_sem=recv_sem,
                device_id=target, device_id_type=MESH,
            ).start()

    def arrived(ref, sem):
        pltpu.make_async_copy(ref, ref, sem).wait()

    barrier = pltpu.get_barrier_semaphore()

    def greet(index, carry):
        @pl.when(index != me)
        def _():
            pl.semaphore_signal(barrier, inc=1, device_id=device(index), device_id_type=MESH)
        return carry

    lax.fori_loop(0, device_count, greet, 0)
    pl.semaphore_wait(barrier, device_count - 1)

    def key_copies(act):
        def one(index, carry):
            s, h = index // heads, index % heads
            column = pl.ds(pl.multiple_of((h * srv + v) * HEAD_SIZE, HEAD_SIZE), HEAD_SIZE)
            start = first + home * s
            here = (s == z) & (h == x)
            full = (base >= start) & (base + rows <= start + window)

            def both(at, count, slot):
                row = pl.multiple_of(base + at - start, chunk)
                for which, ref in ((0, k_ref), (1, v_ref)):
                    act(
                        here,
                        ref.at[pl.ds(pl.multiple_of(at, chunk), count), column],
                        kv_buf.at[which, pl.ds(row, count), :],
                        kv_sem.at[index, slot, which],
                        kv_got.at[which],
                        (s, h, v),
                    )

            @pl.when(full)
            def _():
                both(0, rows, 0)

            def part(c, inner):
                row = base + c * chunk
                @pl.when(jnp.logical_not(full) & (row >= start) & (row + chunk <= start + window))
                def _():
                    both(c * chunk, chunk, c)
                return inner

            lax.fori_loop(0, chunks, part, 0)
            return carry

        lax.fori_loop(0, dp * heads, one, 0)

    def sent(here, src, dst, send_sem, recv_sem, target):
        @pl.when(jnp.logical_not(here))
        def _():
            pltpu.make_async_remote_copy(
                src_ref=src, dst_ref=dst, send_sem=send_sem, recv_sem=recv_sem,
                device_id=target, device_id_type=MESH,
            ).wait_send()

    def doc_copies(act):
        for s in range(dp):
            act(z == s, doc_ref, docs.at[z], doc_sem.at[s], doc_got.at[z], (s, x, v))

    def query_copies(act):
        for u in range(srv):
            act(v == u, qd_ref.at[u], qd_buf.at[v], q_sem.at[u], q_got.at[v], (z, x, u))

    doc_copies(send)
    key_copies(send)
    query_copies(send)

    grad_out[:, pl.ds(0, pad), :] = jnp.zeros((2, pad, HEAD_SIZE), jnp.bfloat16)
    grad_out[:, pl.ds(pad + window, piece), :] = jnp.zeros((2, piece, HEAD_SIZE), jnp.bfloat16)
    acc[...] = jnp.zeros_like(acc)
    total[...] = jnp.zeros_like(total)

    for s in range(dp):
        arrived(docs.at[s], doc_got.at[s])
    blocks = rows * heads // 128
    own = (low + window - home) // 128
    query_doc = docs[own // blocks, pl.ds(own % blocks, 1), :]
    query_at = lax.broadcasted_iota(jnp.int32, (128, home), 1) + (low + window - home)
    for b in range(window // 128):
        index = low // 128 + b
        key_doc = docs[index // blocks, pl.ds(index % blocks, 1), :]
        key_doc = jnp.broadcast_to(key_doc.astype(jnp.float32), (128, 128)).T
        key_at = lax.broadcasted_iota(jnp.int32, (128, home), 0) + (low + b * 128)
        same = key_doc == jnp.broadcast_to(query_doc.astype(jnp.float32), (128, home))
        allowed = same & (key_at <= query_at)
        tile = jnp.where(allowed, 0.0, NEGATIVE)
        for j in range(pair):
            bias[pl.ds(b * 128, 128), pl.ds(j * home, home)] = tile

    arrived(kv_buf.at[0], kv_got.at[0])
    arrived(kv_buf.at[1], kv_got.at[1])
    kt_buf[...] = kv_buf[0].astype(jnp.float32).T.astype(jnp.bfloat16)
    vt_buf[...] = kv_buf[1].astype(jnp.float32).T.astype(jnp.bfloat16)
    for u in range(srv):
        arrived(qd_buf.at[u], q_got.at[u])

    def contract(a, b, left, right):
        return lax.dot_general(a, b, (((left,), (right,)), ((), ())), preferred_element_type=jnp.float32)

    def att_copy(act, u):
        act(v == u, att_out.at[u], att_ref.at[v], att_sem.at[u], att_got.at[v], (z, x, u))

    def dq_copy(act, u):
        act(v == u, dq_out.at[u], dq_ref.at[v], dq_sem.at[u], dq_got.at[v], (z, x, u))

    def heads_step(u, carry):
        query = qd_buf[u, 0].reshape(wide, HEAD_SIZE)
        grad = qd_buf[u, 1].reshape(wide, HEAD_SIZE)
        scores = contract(kv_buf[0], query, 1, 1) + bias[...]
        top = jnp.max(scores, axis=0, keepdims=True)
        weights = jnp.exp2((scores - top) * (scale * math.log2(math.e)))
        norm = jnp.sum(weights, axis=0, keepdims=True)
        out = contract(vt_buf[...], weights.astype(jnp.bfloat16), 1, 0)
        inverse = 1.0 / norm
        out = (out * inverse).astype(jnp.bfloat16).astype(jnp.float32)
        delta = jnp.sum(grad.astype(jnp.float32).T * out, axis=0, keepdims=True)
        att_out[u] = out.T.astype(jnp.bfloat16).reshape(pair, home, HEAD_SIZE)
        att_copy(send, u)
        probs = weights * inverse
        weight_grad = contract(kv_buf[1], grad, 1, 1)
        score_grad = (probs * (weight_grad - delta)).astype(jnp.bfloat16)
        query_grad = contract(kt_buf[...], score_grad, 1, 0) * scale
        dq_out[u] = query_grad.T.astype(jnp.bfloat16).reshape(pair, home, HEAD_SIZE)
        dq_copy(send, u)
        acc[0] += contract(score_grad, query, 1, 0)
        acc[1] += contract(probs.astype(jnp.bfloat16), grad, 1, 0)
        return carry

    lax.fori_loop(0, srv, heads_step, 0)
    grad_out[0, pl.ds(pad, window), :] = (acc[0] * scale).astype(jnp.bfloat16)
    grad_out[1, pl.ds(pad, window), :] = acc[1].astype(jnp.bfloat16)

    lane = x * srv + v
    pieces = window // piece + 2

    def grad_copies(act):
        def one(j, carry):
            owner = low // piece + j
            @pl.when(owner * piece < low + window)
            def _():
                at = pl.multiple_of(owner * piece - low + pad, 16)
                act(
                    owner == me,
                    grad_out.at[:, pl.ds(at, piece), :],
                    grad_in.at[z, lane],
                    g_sem.at[j],
                    g_got.at[z, lane],
                    device(owner),
                )
            return carry

        lax.fori_loop(0, pieces, one, 0)

    grad_copies(send)

    def gather(s, carry):
        start = first + home * s
        @pl.when((me * piece + piece > start) & (me * piece < start + window))
        def _():
            for lane_from in range(heads * srv):
                arrived(grad_in.at[s, lane_from], g_got.at[s, lane_from])
                total[lane_from] += grad_in[s, lane_from].astype(jnp.float32)
        return carry

    lax.fori_loop(0, dp, gather, 0)
    for lane_from in range(heads * srv):
        column = pl.ds(lane_from * HEAD_SIZE, HEAD_SIZE)
        kg_ref[:, column] = total[lane_from, 0].astype(jnp.bfloat16)
        vg_ref[:, column] = total[lane_from, 1].astype(jnp.bfloat16)

    for u in range(srv):
        arrived(att_ref.at[u], att_got.at[u])
        arrived(dq_ref.at[u], dq_got.at[u])
    doc_copies(sent)
    key_copies(sent)
    query_copies(sent)
    for u in range(srv):
        att_copy(sent, u)
        dq_copy(sent, u)
    grad_copies(sent)


def local_window(mesh_sizes, queries, keys, values, output_gradient, doc_ids):
    dp, heads, srv = mesh_sizes
    home, pair, width = queries.shape
    groups = width // HEAD_SIZE
    rows = keys.shape[0]
    key_total = rows * dp * heads
    longest = key_total // 2
    first = key_total - dp * home - longest
    window = longest + home
    piece = rows // srv
    pieces = window // piece + 2
    chunks = rows // math.gcd(home, rows)

    def by_group(array):
        return array.reshape(home, pair, groups, HEAD_SIZE).transpose(2, 1, 0, 3)

    both = jnp.stack([by_group(queries), by_group(output_gradient)], axis=1)
    docs = doc_ids.reshape(-1, 128)
    doc_rows = -(-docs.shape[0] // 8) * 8
    docs = jnp.pad(docs, ((0, doc_rows - docs.shape[0]), (0, 0)))
    vmem = pl.BlockSpec(memory_space=pltpu.VMEM)
    anywhere = pl.BlockSpec(memory_space=pl.ANY)
    sem = pltpu.SemaphoreType.DMA
    lanes = heads * srv
    b16, f32 = jnp.bfloat16, jnp.float32
    sizes = (dp, heads, srv, home, pair, rows, first, window)
    att, dq, kg, vg = pl.pallas_call(
        functools.partial(attend, sizes),
        out_shape=(
            jax.ShapeDtypeStruct((groups, pair, home, HEAD_SIZE), b16),
            jax.ShapeDtypeStruct((groups, pair, home, HEAD_SIZE), b16),
            jax.ShapeDtypeStruct((piece, lanes * HEAD_SIZE), b16),
            jax.ShapeDtypeStruct((piece, lanes * HEAD_SIZE), b16),
        ),
        in_specs=[anywhere] * 4,
        out_specs=(vmem, vmem, vmem, vmem),
        scratch_shapes=[
            pltpu.VMEM((srv, 2, pair, home, HEAD_SIZE), b16),
            pltpu.VMEM((2, window, HEAD_SIZE), b16),
            pltpu.VMEM((HEAD_SIZE, window), b16),
            pltpu.VMEM((HEAD_SIZE, window), b16),
            pltpu.VMEM((dp, doc_rows, 128), jnp.int32),
            pltpu.VMEM((window, pair * home), f32),
            pltpu.VMEM((2, window, HEAD_SIZE), f32),
            pltpu.VMEM((2, window + 2 * piece, HEAD_SIZE), b16),
            pltpu.VMEM((srv, pair, home, HEAD_SIZE), b16),
            pltpu.VMEM((srv, pair, home, HEAD_SIZE), b16),
            pltpu.VMEM((dp, lanes, 2, piece, HEAD_SIZE), b16),
            pltpu.VMEM((lanes, 2, piece, HEAD_SIZE), f32),
            sem((srv,)), sem((srv,)),
            sem((dp * heads, chunks, 2)), sem((2,)),
            sem((dp,)), sem((dp,)),
            sem((srv,)), sem((srv,)),
            sem((srv,)), sem((srv,)),
            sem((pieces,)), sem((dp, lanes)),
        ],
        compiler_params=pltpu.CompilerParams(
            collective_id=0, has_side_effects=True, vmem_limit_bytes=48 * 1024 * 1024
        ),
    )(both, keys, values, docs)

    def by_row(array):
        return array.transpose(2, 1, 0, 3).reshape(home, pair, width)

    return by_row(att), by_row(dq), kg, vg


def local_spread(queries, keys, values, output_gradient, doc_ids):
    home_rows, pair_heads, group_width = queries.shape
    groups = group_width // HEAD_SIZE
    scale_factor = HEAD_SIZE ** (-0.5)
    key_rows, value_rows = (
        lax.all_to_all(keys, "head", split_axis=1, concat_axis=0, tiled=True),
        lax.all_to_all(values, "head", split_axis=1, concat_axis=0, tiled=True),
    )
    key_count = key_rows.shape[0]
    servers = lax.axis_size("dp")
    server = lax.axis_index("dp")
    key_at = server * key_count + jnp.arange(key_count, dtype=jnp.int32)
    all_docs = lax.all_gather(doc_ids, "dp", axis=0, tiled=True)
    query_total = home_rows * servers
    context = all_docs.shape[0] - query_total
    query_docs = all_docs[context:]
    query_places = context + jnp.arange(query_total, dtype=jnp.int32)
    all_q, all_dout = (
        lax.all_gather(queries, "dp", axis=0, tiled=True),
        lax.all_gather(output_gradient, "dp", axis=0, tiled=True),
    )
    block_rows = math.gcd(512, query_total)
    block_count = query_total // block_rows
    key_heads = key_rows.reshape(key_count, groups, HEAD_SIZE)
    value_heads = value_rows.reshape(key_count, groups, HEAD_SIZE)
    query_blocks = all_q.reshape(block_count, block_rows, pair_heads, groups, HEAD_SIZE)
    grad_blocks = all_dout.reshape(block_count, block_rows, pair_heads, groups, HEAD_SIZE)
    place_blocks = query_places.reshape(block_count, block_rows)
    doc_blocks = query_docs.reshape(block_count, block_rows)

    def admissible(places, query_doc):
        return (key_at[None, :] <= places[:, None]) & (doc_ids[None, :] == query_doc[:, None])

    def scores_of(query_block):
        return (
            jnp.einsum("pjgd,kgd->gjpk", query_block, key_heads, preferred_element_type=jnp.float32)
            * scale_factor
        )

    def block_max(inputs):
        query_block, places, query_doc = inputs
        allowed = admissible(places, query_doc)

        def compute():
            raw_scores = scores_of(query_block)
            masked = jnp.where(allowed[None, None], raw_scores, NEGATIVE)
            return (jnp.max(masked, axis=-1).transpose(2, 1, 0), raw_scores)

        return compute()

    def block_top(inputs):
        return block_max(inputs)[0]

    local_max = lax.map(block_top, (query_blocks, place_blocks, doc_blocks))
    row_max = lax.pmax(local_max.reshape(query_total, pair_heads, groups), "dp")
    max_blocks = row_max.reshape(block_count, block_rows, pair_heads, groups)

    def block_sum(inputs):
        stored, places, query_doc, row_top = inputs
        allowed = admissible(places, query_doc)

        def compute():
            block_scores = scores_of(stored)
            shifted = block_scores - row_top.transpose(2, 1, 0)[..., None]
            weights = jnp.where(allowed[None, None], jnp.exp(shifted), 0.0)
            weighted = jnp.einsum(
                "gjpk,kgd->pjgd",
                weights.astype(jnp.bfloat16),
                value_heads,
                preferred_element_type=jnp.float32,
            )
            return (
                weighted.reshape(block_rows, pair_heads, group_width),
                jnp.sum(weights, axis=-1).transpose(2, 1, 0),
            )

        return compute()

    part_out, part_norm = lax.map(block_sum, (query_blocks, place_blocks, doc_blocks, max_blocks))
    part_out = part_out.reshape(query_total, pair_heads, group_width)
    part_norm = part_norm.reshape(query_total, pair_heads, groups)
    home_out, home_norm = (
        lax.psum_scatter(part_out, "dp", scatter_dimension=0, tiled=True),
        lax.psum_scatter(part_norm, "dp", scatter_dimension=0, tiled=True),
    )
    home_max = lax.dynamic_slice_in_dim(row_max, server * home_rows, home_rows, 0)
    attn_home = (
        home_out.reshape(home_rows, pair_heads, groups, HEAD_SIZE) / home_norm[..., None]
    ).astype(jnp.bfloat16)
    log_home = home_max + jnp.log(home_norm)
    grad_home = output_gradient.reshape(home_rows, pair_heads, groups, HEAD_SIZE).astype(
        jnp.float32
    )
    delta_home = jnp.sum(grad_home * attn_home.astype(jnp.float32), axis=-1)
    log_all, delta_all = (
        lax.all_gather(log_home, "dp", axis=0, tiled=True),
        lax.all_gather(delta_home, "dp", axis=0, tiled=True),
    )
    attention = attn_home.reshape(home_rows, pair_heads, group_width)
    log_blocks = log_all.reshape(block_count, block_rows, pair_heads, groups)
    delta_blocks = delta_all.reshape(block_count, block_rows, pair_heads, groups)

    def block_grad(totals, inputs):
        query_block, grad_block, places, query_doc, log_norm, row_delta = inputs
        allowed = admissible(places, query_doc)

        def compute():
            shifted = scores_of(query_block) - log_norm.transpose(2, 1, 0)[..., None]
            probs = jnp.where(allowed[None, None], jnp.exp(shifted), 0.0)
            value_grad = jnp.einsum(
                "gjpk,pjgd->kgd",
                probs.astype(jnp.bfloat16),
                grad_block,
                preferred_element_type=jnp.float32,
            )
            weight_grad = jnp.einsum(
                "pjgd,kgd->gjpk", grad_block, value_heads, preferred_element_type=jnp.float32
            )
            score_grad = (probs * (weight_grad - row_delta.transpose(2, 1, 0)[..., None])).astype(
                jnp.bfloat16
            )
            query_grad = (
                jnp.einsum(
                    "gjpk,kgd->pjgd", score_grad, key_heads, preferred_element_type=jnp.float32
                )
                * scale_factor
            )
            key_grad = (
                jnp.einsum(
                    "gjpk,pjgd->kgd", score_grad, query_block, preferred_element_type=jnp.float32
                )
                * scale_factor
            )
            return (query_grad.reshape(block_rows, pair_heads, group_width), key_grad, value_grad)

        query_grad, key_grad, value_grad = compute()
        return ((totals[0] + key_grad, totals[1] + value_grad), query_grad)

    zero_start = jnp.zeros((key_count, groups, HEAD_SIZE), jnp.float32)
    grad_inputs = (query_blocks, grad_blocks, place_blocks, doc_blocks, log_blocks, delta_blocks)
    (key_total, value_total), query_parts = lax.scan(
        block_grad, (zero_start, zero_start), grad_inputs
    )
    q_summed = lax.psum_scatter(
        query_parts.reshape(query_total, pair_heads, group_width).astype(jnp.bfloat16),
        "dp",
        scatter_dimension=0,
        tiled=True,
    )
    spread_key, spread_value = (
        lax.all_to_all(
            key_total.reshape(key_count, group_width).astype(jnp.bfloat16),
            "head",
            split_axis=0,
            concat_axis=1,
            tiled=True,
        ).astype(jnp.float32),
        lax.all_to_all(
            value_total.reshape(key_count, group_width).astype(jnp.bfloat16),
            "head",
            split_axis=0,
            concat_axis=1,
            tiled=True,
        ).astype(jnp.float32),
    )
    k_summed, v_summed = (
        lax.psum_scatter(
            spread_key.astype(jnp.bfloat16), "srv", scatter_dimension=0, tiled=True
        ).astype(jnp.float32),
        lax.psum_scatter(
            spread_value.astype(jnp.bfloat16), "srv", scatter_dimension=0, tiled=True
        ).astype(jnp.float32),
    )
    return (attention, q_summed, k_summed.astype(jnp.bfloat16), v_summed.astype(jnp.bfloat16))


def solution(mesh):
    placed = (
        P("dp", "srv", "head"),
        P(("dp", "head"), None),
        P(("dp", "head"), None),
        P("dp", "srv", "head"),
        P("dp"),
    )
    sizes = tuple(mesh.shape[name] for name in AXES)

    def local(queries, keys, values, output_gradient, doc_ids):
        args = (queries, keys, values, output_gradient, doc_ids)
        if queries.shape[2] == sizes[2] * HEAD_SIZE:
            return local_window(sizes, *args)
        return local_spread(*args)

    return jax.shard_map(
        local,
        mesh=mesh,
        in_specs=placed,
        out_specs=(
            P("dp", "srv", "head"),
            P("dp", "srv", "head"),
            P(("dp", "head", "srv"), None),
            P(("dp", "head", "srv"), None),
        ),
        check_vma=False,
    )
```

```python
import functools
import math

import jax
import jax.numpy as jnp
from jax import lax
from jax.experimental import pallas as pl
from jax.experimental.pallas import tpu as pltpu
from jax.sharding import PartitionSpec as P

HEAD_SIZE = 128


NEGATIVE = -1e30
MESH = pl.DeviceIdType.MESH
AXES = ("dp", "head", "srv")


TILE = 128


def attend(sizes, qd_ref, k_ref, v_ref, doc_ref, att_ref, dq_ref, g_ref,
           qd_buf, kv_buf, docs, scores, top, norm, out_t, dq_t, acc, part, up_in, down_in, owned, att_out, dq_out,
           q_sem, q_got, kv_sem, kv_got, relay_sem, doc_sem, doc_got, att_sem, att_got, dq_sem, dq_got,
           part_sem, up_got, down_got, g_sem, g_got):
    dp, heads, srv, home, pair, rows, first, window = sizes
    chunk = math.gcd(TILE, rows)
    chunks = rows // chunk
    piece = rows // srv
    wide = pair * home
    every = srv * wide
    tiles = window // TILE
    blocks = rows * heads // TILE
    lanes = heads * srv
    scale = HEAD_SIZE ** (-0.5)
    exponent = scale * math.log2(math.e)
    z, x, v = (lax.axis_index(name) for name in AXES)
    base = (z * heads + x) * rows
    low = first + home * z
    low_tile = low // TILE
    own_first = jnp.maximum(z * blocks - low_tile, 0)
    lane = x * srv + v

    def copy(src, dst, send_sem, recv_sem, target):
        return pltpu.make_async_remote_copy(
            src_ref=src, dst_ref=dst, send_sem=send_sem, recv_sem=recv_sem,
            device_id=target, device_id_type=MESH,
        )

    def send(here, src, dst, send_sem, recv_sem, target):
        @pl.when(here)
        def _():
            pltpu.make_async_copy(src, dst, recv_sem).start()

        @pl.when(jnp.logical_not(here))
        def _():
            copy(src, dst, send_sem, recv_sem, target).start()

    def sent(here, src, dst, send_sem, recv_sem, target):
        @pl.when(jnp.logical_not(here))
        def _():
            copy(src, dst, send_sem, recv_sem, target).wait_send()

    def arrived(ref, sem):
        pltpu.make_async_copy(ref, ref, sem).wait()

    barrier = pltpu.get_barrier_semaphore()

    def greet(index, carry):
        s, h, u = index // lanes, (index // srv) % heads, index % srv
        beside = (s - z == 1) | (z - s == 1)
        partner = (s == z) | ((u == v) & (beside | (h == x)))
        myself = (s == z) & (h == x) & (u == v)

        @pl.when(partner & jnp.logical_not(myself))
        def _():
            pl.semaphore_signal(barrier, inc=1, device_id=(s, h, u), device_id_type=MESH)
        return carry

    lax.fori_loop(0, dp * lanes, greet, 0)
    sides = jnp.where(z > 0, 1, 0) + jnp.where(z < dp - 1, 1, 0)
    pl.semaphore_wait(barrier, lanes - 1 + sides * heads + dp - 1 - sides)

    def key_copies(act):
        def one(index, carry):
            side, h = index // heads, index % heads
            s = z + jnp.where(side == 0, -1, jnp.where(side == 1, 1, 0))
            column = pl.ds(pl.multiple_of((h * srv + v) * HEAD_SIZE, HEAD_SIZE), HEAD_SIZE)
            start = first + home * s

            def each(c, inner):
                row = base + c * chunk - start

                @pl.when((s >= 0) & (s < dp) & (row >= 0) & (row < window))
                def _():
                    for which, ref in ((0, k_ref), (1, v_ref)):
                        act(
                            (s == z) & (h == x),
                            ref.at[pl.ds(pl.multiple_of(c * chunk, chunk), chunk), column],
                            kv_buf.at[row // TILE, which, pl.ds(pl.multiple_of(row % TILE, chunk), chunk), :],
                            kv_sem.at[index, c, which],
                            kv_got.at[row // TILE],
                            (s, h, v),
                        )
                return inner

            lax.fori_loop(0, chunks, each, 0)
            return carry

        lax.fori_loop(0, 3 * heads, one, 0)

    def doc_copies(act):
        for s in range(dp):
            act(z == s, doc_ref, docs.at[z], doc_sem.at[s], doc_got.at[z], (s, x, v))

    def query_copies(act):
        for u in range(srv):
            act(v == u, qd_ref.at[u], qd_buf.at[:, v], q_sem.at[u], q_got.at[v], (z, x, u))

    doc_copies(send)
    query_copies(send)
    key_copies(send)

    top[...] = jnp.full_like(top, NEGATIVE / 10)
    norm[...] = jnp.zeros_like(norm)
    out_t[...] = jnp.zeros_like(out_t)
    dq_t[...] = jnp.zeros_like(dq_t)
    owned[...] = jnp.zeros_like(owned)

    def contract(a, b, left, right):
        return lax.dot_general(a, b, (((left,), (right,)), ((), ())), preferred_element_type=jnp.float32)

    def turned(a):
        return a.astype(jnp.float32).T.astype(jnp.bfloat16)

    for s in range(dp):
        arrived(docs.at[s], doc_got.at[s])
    home_tile = low_tile + tiles - 1
    query_doc = docs[home_tile // blocks, pl.ds(home_tile % blocks, 1), :]
    query_doc = jnp.broadcast_to(query_doc.astype(jnp.float32), (TILE, home))
    query_at = lax.broadcasted_iota(jnp.int32, (TILE, home), 1) + home_tile * TILE
    for u in range(srv):
        arrived(qd_buf.at[:, u], q_got.at[u])

    def relays(act, tile):
        shard = (low_tile + tile) // blocks

        @pl.when((shard > z) & (z > 0) & (tile < tiles - 1))
        def _():
            act(copy(kv_buf.at[tile], kv_buf.at[tile + 1], relay_sem.at[tile], kv_got.at[tile + 1], (z - 1, x, v)))

        @pl.when((shard < z) & (z < dp - 1) & (tile > 0))
        def _():
            act(copy(kv_buf.at[tile], kv_buf.at[tile - 1], relay_sem.at[tile], kv_got.at[tile - 1], (z + 1, x, v)))

    def forward(i, carry):
        tile = jnp.where(i < tiles - own_first, own_first + i, tiles - 1 - i)
        index = low_tile + tile
        arrived(kv_buf.at[tile], kv_got.at[tile])
        relays(lambda c: c.start(), tile)
        key_doc = docs[index // blocks, pl.ds(index % blocks, 1), :]
        key_doc = jnp.broadcast_to(key_doc.astype(jnp.float32), (TILE, TILE)).T
        key_at = lax.broadcasted_iota(jnp.int32, (TILE, home), 0) + index * TILE
        bias = jnp.where((key_doc == query_doc) & (key_at <= query_at), 0.0, NEGATIVE)
        value_t = turned(kv_buf[tile, 1])
        keys = kv_buf[tile, 0]
        for u in range(srv):
            at = pl.ds(u * wide, wide)
            raw = contract(keys, qd_buf[0, u], 1, 1) + jnp.concatenate([bias] * pair, axis=1)
            scores[tile, :, at] = raw
            old = top[:, at]
            new = jnp.maximum(old, jnp.max(raw, axis=0, keepdims=True))
            weights = jnp.exp2((raw - new) * exponent)
            shrink = jnp.exp2((old - new) * exponent)
            top[:, at] = new
            norm[:, at] = norm[:, at] * shrink + jnp.sum(weights, axis=0, keepdims=True)
            out_t[:, at] = out_t[:, at] * shrink + contract(value_t, weights.astype(jnp.bfloat16), 1, 0)
        return carry

    lax.fori_loop(0, tiles, forward, 0)

    def att_copy(act, u):
        act(v == u, att_out.at[u], att_ref.at[v], att_sem.at[u], att_got.at[v], (z, x, u))

    def dq_copy(act, u):
        act(v == u, dq_out.at[u], dq_ref.at[v], dq_sem.at[u], dq_got.at[v], (z, x, u))

    for u in range(srv):
        at = pl.ds(u * wide, wide)
        out = (out_t[:, at] / norm[:, at]).T.astype(jnp.bfloat16)
        att_out[u] = out
        att_copy(send, u)
        product = qd_buf[1, u].astype(jnp.float32) * out.astype(jnp.float32)
        out_t[pl.ds(0, 1), at] = jnp.sum(product.T, axis=0, keepdims=True)
        top[:, at] = top[:, at] * exponent + jnp.log2(norm[:, at])

    def part_copies(act, tile):
        shard = (low_tile + tile) // blocks

        @pl.when(shard > z)
        def _():
            act(copy(part.at[tile], up_in.at[tile], part_sem.at[tile], up_got.at[tile], (z + 1, x, v)))

        @pl.when(shard < z)
        def _():
            act(copy(part.at[tile], down_in.at[tile], part_sem.at[tile], down_got.at[tile], (z - 1, x, v)))

    def backward(i, carry):
        tile = jnp.where(i == 0, tiles - 1, jnp.where(i <= own_first, i - 1, tiles - 1 + own_first - i))
        index = low_tile + tile
        shard = index // blocks
        key_t = turned(kv_buf[tile, 0])
        values = kv_buf[tile, 1]
        key_grad = jnp.zeros((TILE, HEAD_SIZE), jnp.float32)
        value_grad = jnp.zeros((TILE, HEAD_SIZE), jnp.float32)
        for u in range(srv):
            at = pl.ds(u * wide, wide)
            probs = jnp.exp2(scores[tile, :, at] * exponent - top[:, at])
            weight_grad = contract(values, qd_buf[1, u], 1, 1)
            score_grad = (probs * (weight_grad - out_t[pl.ds(0, 1), at])).astype(jnp.bfloat16)
            key_grad = key_grad + contract(score_grad, qd_buf[0, u], 1, 0)
            value_grad = value_grad + contract(probs.astype(jnp.bfloat16), qd_buf[1, u], 1, 0)
            dq_t[:, at] += contract(key_t, score_grad, 1, 0)
        acc[0] = key_grad * scale
        acc[1] = value_grad

        @pl.when((shard >= z) & (z > 0) & (tile < tiles - 1))
        def _():
            arrived(up_in.at[tile + 1], up_got.at[tile + 1])
            acc[...] += up_in[tile + 1].astype(jnp.float32)

        @pl.when((shard <= z) & (z < dp - 1) & (tile > 0))
        def _():
            arrived(down_in.at[tile - 1], down_got.at[tile - 1])
            acc[...] += down_in[tile - 1].astype(jnp.float32)

        @pl.when(shard == z)
        def _():
            owned[:, pl.ds(pl.multiple_of((index - z * blocks) * TILE, TILE), TILE), :] = acc[...].astype(jnp.bfloat16)

        @pl.when(shard != z)
        def _():
            part[tile] = acc[...].astype(jnp.bfloat16)
        part_copies(lambda c: c.start(), tile)
        return carry

    lax.fori_loop(0, tiles, backward, 0)

    @pl.when((z > 0) & ((low_tile - 1) // blocks == z))
    def _():
        arrived(up_in.at[0], up_got.at[0])
        owned[:, pl.ds(pl.multiple_of((low_tile - 1 - z * blocks) * TILE, TILE), TILE), :] = up_in[0]

    def grad_copies(act):
        column = pl.ds(pl.multiple_of(lane * HEAD_SIZE, HEAD_SIZE), HEAD_SIZE)
        for j in range(lanes):
            act(
                lane == j,
                owned.at[:, pl.ds(j * piece, piece), :],
                g_ref.at[:, :, column],
                g_sem.at[j],
                g_got.at[lane],
                (z, j // srv, j % srv),
            )

    grad_copies(send)
    for u in range(srv):
        dq_out[u] = (dq_t[:, pl.ds(u * wide, wide)] * scale).T.astype(jnp.bfloat16)
        dq_copy(send, u)

    doc_copies(sent)
    key_copies(sent)
    query_copies(sent)

    def settle(tile, carry):
        relays(lambda c: c.wait_send(), tile)
        part_copies(lambda c: c.wait_send(), tile)
        return carry

    lax.fori_loop(0, tiles, settle, 0)
    for u in range(srv):
        att_copy(sent, u)
        arrived(att_ref.at[u], att_got.at[u])
    for u in range(srv):
        dq_copy(sent, u)
        arrived(dq_ref.at[u], dq_got.at[u])
    grad_copies(sent)
    for j in range(lanes):
        arrived(g_ref.at[:, :, pl.ds(j * HEAD_SIZE, HEAD_SIZE)], g_got.at[j])


def window_sizes(mesh_sizes, queries, keys):
    dp, heads, srv = mesh_sizes
    home, pair, width = queries.shape
    rows = keys.shape[0]
    key_total = rows * dp * heads
    longest = key_total // 2
    first = key_total - dp * home - longest
    return (dp, heads, srv, home, pair, rows, first, longest + home)


def window_fits(sizes, width):
    dp, heads, srv, home, pair, rows, first, window = sizes
    shard = rows * heads
    if width != srv * HEAD_SIZE or home != TILE or shard % TILE or first < 0 or first % TILE or window % TILE:
        return False
    if rows % srv or (rows // srv) % 16 or rows % 16:
        return False
    blocks, tiles, start = shard // TILE, window // TILE, first // TILE
    for s in range(dp):
        held = set(range(start + s, start + s + tiles))
        for other in (s - 1, s + 1):
            if 0 <= other < dp:
                for tile in range(start + other, start + other + tiles):
                    beyond = tile // blocks > s if other < s else tile // blocks < s
                    owned = tile // blocks == s
                    if (beyond or owned) and tile not in held and not (owned and other < s and tile == start + other):
                        return False
                    through = tile // blocks > s if other < s else tile // blocks < s
                    if through and tile not in held:
                        return False
    return True


def local_window(sizes, queries, keys, values, output_gradient, doc_ids):
    dp, heads, srv, home, pair, rows, first, window = sizes
    width = queries.shape[2]
    groups = width // HEAD_SIZE
    wide = pair * home
    tiles = window // TILE
    piece = rows // srv
    chunks = rows // math.gcd(TILE, rows)

    def by_group(array):
        return array.reshape(home, pair, groups, HEAD_SIZE).transpose(2, 1, 0, 3).reshape(groups, wide, HEAD_SIZE)

    both = jnp.stack([by_group(queries), by_group(output_gradient)], axis=1)
    docs = doc_ids.reshape(-1, TILE)
    doc_rows = -(-docs.shape[0] // 8) * 8
    docs = jnp.pad(docs, ((0, doc_rows - docs.shape[0]), (0, 0)))
    vmem = pl.BlockSpec(memory_space=pltpu.VMEM)
    anywhere = pl.BlockSpec(memory_space=pl.ANY)
    sem = pltpu.SemaphoreType.DMA
    lanes = heads * srv
    b16, f32 = jnp.bfloat16, jnp.float32
    att, dq, kv = pl.pallas_call(
        functools.partial(attend, sizes),
        out_shape=(
            jax.ShapeDtypeStruct((groups, wide, HEAD_SIZE), b16),
            jax.ShapeDtypeStruct((groups, wide, HEAD_SIZE), b16),
            jax.ShapeDtypeStruct((2, piece, lanes * HEAD_SIZE), b16),
        ),
        in_specs=[anywhere] * 4,
        out_specs=(vmem, vmem, vmem),
        scratch_shapes=[
            pltpu.VMEM((2, srv, wide, HEAD_SIZE), b16),
            pltpu.VMEM((tiles, 2, TILE, HEAD_SIZE), b16),
            pltpu.VMEM((dp, doc_rows, TILE), jnp.int32),
            pltpu.VMEM((tiles, TILE, srv * wide), f32),
            pltpu.VMEM((1, srv * wide), f32),
            pltpu.VMEM((1, srv * wide), f32),
            pltpu.VMEM((HEAD_SIZE, srv * wide), f32),
            pltpu.VMEM((HEAD_SIZE, srv * wide), f32),
            pltpu.VMEM((2, TILE, HEAD_SIZE), f32),
            pltpu.VMEM((tiles, 2, TILE, HEAD_SIZE), b16),
            pltpu.VMEM((tiles, 2, TILE, HEAD_SIZE), b16),
            pltpu.VMEM((tiles, 2, TILE, HEAD_SIZE), b16),
            pltpu.VMEM((2, rows * heads, HEAD_SIZE), b16),
            pltpu.VMEM((srv, wide, HEAD_SIZE), b16),
            pltpu.VMEM((srv, wide, HEAD_SIZE), b16),
            sem((srv,)), sem((srv,)),
            sem((3 * heads, chunks, 2)), sem((tiles,)), sem((tiles,)),
            sem((dp,)), sem((dp,)),
            sem((srv,)), sem((srv,)),
            sem((srv,)), sem((srv,)),
            sem((tiles,)), sem((tiles,)), sem((tiles,)),
            sem((lanes,)), sem((lanes,)),
        ],
        compiler_params=pltpu.CompilerParams(
            collective_id=0, has_side_effects=True, vmem_limit_bytes=40 * 1024 * 1024
        ),
    )(both, keys, values, docs)

    def by_row(array):
        return array.reshape(groups, pair, home, HEAD_SIZE).transpose(2, 1, 0, 3).reshape(home, pair, width)

    return by_row(att), by_row(dq), kv[0], kv[1]


def local_spread(queries, keys, values, output_gradient, doc_ids):
    home_rows, pair_heads, group_width = queries.shape
    groups = group_width // HEAD_SIZE
    scale_factor = HEAD_SIZE ** (-0.5)
    key_rows, value_rows = (
        lax.all_to_all(keys, "head", split_axis=1, concat_axis=0, tiled=True),
        lax.all_to_all(values, "head", split_axis=1, concat_axis=0, tiled=True),
    )
    key_count = key_rows.shape[0]
    servers = lax.axis_size("dp")
    server = lax.axis_index("dp")
    key_at = server * key_count + jnp.arange(key_count, dtype=jnp.int32)
    all_docs = lax.all_gather(doc_ids, "dp", axis=0, tiled=True)
    query_total = home_rows * servers
    context = all_docs.shape[0] - query_total
    query_docs = all_docs[context:]
    query_places = context + jnp.arange(query_total, dtype=jnp.int32)
    all_q, all_dout = (
        lax.all_gather(queries, "dp", axis=0, tiled=True),
        lax.all_gather(output_gradient, "dp", axis=0, tiled=True),
    )
    block_rows = math.gcd(512, query_total)
    block_count = query_total // block_rows
    key_heads = key_rows.reshape(key_count, groups, HEAD_SIZE)
    value_heads = value_rows.reshape(key_count, groups, HEAD_SIZE)
    query_blocks = all_q.reshape(block_count, block_rows, pair_heads, groups, HEAD_SIZE)
    grad_blocks = all_dout.reshape(block_count, block_rows, pair_heads, groups, HEAD_SIZE)
    place_blocks = query_places.reshape(block_count, block_rows)
    doc_blocks = query_docs.reshape(block_count, block_rows)

    def admissible(places, query_doc):
        return (key_at[None, :] <= places[:, None]) & (doc_ids[None, :] == query_doc[:, None])

    def scores_of(query_block):
        return (
            jnp.einsum("pjgd,kgd->gjpk", query_block, key_heads, preferred_element_type=jnp.float32)
            * scale_factor
        )

    def block_max(inputs):
        query_block, places, query_doc = inputs
        allowed = admissible(places, query_doc)

        def compute():
            raw_scores = scores_of(query_block)
            masked = jnp.where(allowed[None, None], raw_scores, NEGATIVE)
            return (jnp.max(masked, axis=-1).transpose(2, 1, 0), raw_scores)

        return compute()

    def block_top(inputs):
        return block_max(inputs)[0]

    local_max = lax.map(block_top, (query_blocks, place_blocks, doc_blocks))
    row_max = lax.pmax(local_max.reshape(query_total, pair_heads, groups), "dp")
    max_blocks = row_max.reshape(block_count, block_rows, pair_heads, groups)

    def block_sum(inputs):
        stored, places, query_doc, row_top = inputs
        allowed = admissible(places, query_doc)

        def compute():
            block_scores = scores_of(stored)
            shifted = block_scores - row_top.transpose(2, 1, 0)[..., None]
            weights = jnp.where(allowed[None, None], jnp.exp(shifted), 0.0)
            weighted = jnp.einsum(
                "gjpk,kgd->pjgd",
                weights.astype(jnp.bfloat16),
                value_heads,
                preferred_element_type=jnp.float32,
            )
            return (
                weighted.reshape(block_rows, pair_heads, group_width),
                jnp.sum(weights, axis=-1).transpose(2, 1, 0),
            )

        return compute()

    part_out, part_norm = lax.map(block_sum, (query_blocks, place_blocks, doc_blocks, max_blocks))
    part_out = part_out.reshape(query_total, pair_heads, group_width)
    part_norm = part_norm.reshape(query_total, pair_heads, groups)
    home_out, home_norm = (
        lax.psum_scatter(part_out, "dp", scatter_dimension=0, tiled=True),
        lax.psum_scatter(part_norm, "dp", scatter_dimension=0, tiled=True),
    )
    home_max = lax.dynamic_slice_in_dim(row_max, server * home_rows, home_rows, 0)
    attn_home = (
        home_out.reshape(home_rows, pair_heads, groups, HEAD_SIZE) / home_norm[..., None]
    ).astype(jnp.bfloat16)
    log_home = home_max + jnp.log(home_norm)
    grad_home = output_gradient.reshape(home_rows, pair_heads, groups, HEAD_SIZE).astype(
        jnp.float32
    )
    delta_home = jnp.sum(grad_home * attn_home.astype(jnp.float32), axis=-1)
    log_all, delta_all = (
        lax.all_gather(log_home, "dp", axis=0, tiled=True),
        lax.all_gather(delta_home, "dp", axis=0, tiled=True),
    )
    attention = attn_home.reshape(home_rows, pair_heads, group_width)
    log_blocks = log_all.reshape(block_count, block_rows, pair_heads, groups)
    delta_blocks = delta_all.reshape(block_count, block_rows, pair_heads, groups)

    def block_grad(totals, inputs):
        query_block, grad_block, places, query_doc, log_norm, row_delta = inputs
        allowed = admissible(places, query_doc)

        def compute():
            shifted = scores_of(query_block) - log_norm.transpose(2, 1, 0)[..., None]
            probs = jnp.where(allowed[None, None], jnp.exp(shifted), 0.0)
            value_grad = jnp.einsum(
                "gjpk,pjgd->kgd",
                probs.astype(jnp.bfloat16),
                grad_block,
                preferred_element_type=jnp.float32,
            )
            weight_grad = jnp.einsum(
                "pjgd,kgd->gjpk", grad_block, value_heads, preferred_element_type=jnp.float32
            )
            score_grad = (probs * (weight_grad - row_delta.transpose(2, 1, 0)[..., None])).astype(
                jnp.bfloat16
            )
            query_grad = (
                jnp.einsum(
                    "gjpk,kgd->pjgd", score_grad, key_heads, preferred_element_type=jnp.float32
                )
                * scale_factor
            )
            key_grad = (
                jnp.einsum(
                    "gjpk,pjgd->kgd", score_grad, query_block, preferred_element_type=jnp.float32
                )
                * scale_factor
            )
            return (query_grad.reshape(block_rows, pair_heads, group_width), key_grad, value_grad)

        query_grad, key_grad, value_grad = compute()
        return ((totals[0] + key_grad, totals[1] + value_grad), query_grad)

    zero_start = jnp.zeros((key_count, groups, HEAD_SIZE), jnp.float32)
    grad_inputs = (query_blocks, grad_blocks, place_blocks, doc_blocks, log_blocks, delta_blocks)
    (key_total, value_total), query_parts = lax.scan(
        block_grad, (zero_start, zero_start), grad_inputs
    )
    q_summed = lax.psum_scatter(
        query_parts.reshape(query_total, pair_heads, group_width).astype(jnp.bfloat16),
        "dp",
        scatter_dimension=0,
        tiled=True,
    )
    spread_key, spread_value = (
        lax.all_to_all(
            key_total.reshape(key_count, group_width).astype(jnp.bfloat16),
            "head",
            split_axis=0,
            concat_axis=1,
            tiled=True,
        ).astype(jnp.float32),
        lax.all_to_all(
            value_total.reshape(key_count, group_width).astype(jnp.bfloat16),
            "head",
            split_axis=0,
            concat_axis=1,
            tiled=True,
        ).astype(jnp.float32),
    )
    k_summed, v_summed = (
        lax.psum_scatter(
            spread_key.astype(jnp.bfloat16), "srv", scatter_dimension=0, tiled=True
        ).astype(jnp.float32),
        lax.psum_scatter(
            spread_value.astype(jnp.bfloat16), "srv", scatter_dimension=0, tiled=True
        ).astype(jnp.float32),
    )
    return (attention, q_summed, k_summed.astype(jnp.bfloat16), v_summed.astype(jnp.bfloat16))


def solution(mesh):
    placed = (
        P("dp", "srv", "head"),
        P(("dp", "head"), None),
        P(("dp", "head"), None),
        P("dp", "srv", "head"),
        P("dp"),
    )
    mesh_sizes = tuple(mesh.shape[name] for name in AXES)

    def local(queries, keys, values, output_gradient, doc_ids):
        args = (queries, keys, values, output_gradient, doc_ids)
        sizes = window_sizes(mesh_sizes, queries, keys)
        if window_fits(sizes, queries.shape[2]):
            return local_window(sizes, *args)
        return local_spread(*args)

    return jax.shard_map(
        local,
        mesh=mesh,
        in_specs=placed,
        out_specs=(
            P("dp", "srv", "head"),
            P("dp", "srv", "head"),
            P(("dp", "head", "srv"), None),
            P(("dp", "head", "srv"), None),
        ),
        check_vma=False,
    )
```

```python
import functools
import math

import jax
import jax.numpy as jnp
from jax import lax
from jax.experimental import pallas as pl
from jax.experimental.pallas import tpu as pltpu
from jax.sharding import PartitionSpec as P

HEAD_SIZE = 128


NEGATIVE = -1e30
MESH = pl.DeviceIdType.MESH
AXES = ("dp", "head", "srv")


TILE = 128
LAG = 3


def attend(sizes, qd_ref, k_ref, v_ref, doc_ref, att_ref, dq_ref, g_ref,
           qd_buf, kv_buf, docs, scores, top, norm, delta, out_t, grad_t, dq_t, acc, part, up_in, down_in, owned, att_out, dq_out,
           q_sem, q_got, kv_sem, kv_got, relay_sem, doc_sem, doc_got, att_sem, att_got, dq_sem, dq_got,
           part_sem, up_got, down_got, g_sem, g_got):
    dp, heads, srv, home, pair, rows, first, window = sizes
    chunk = math.gcd(TILE, rows)
    chunks = rows // chunk
    piece = rows // srv
    wide = pair * home
    every = srv * wide
    tiles = window // TILE
    blocks = rows * heads // TILE
    lanes = heads * srv
    scale = HEAD_SIZE ** (-0.5)
    exponent = scale * math.log2(math.e)
    z, x, v = (lax.axis_index(name) for name in AXES)
    base = (z * heads + x) * rows
    low = first + home * z
    low_tile = low // TILE
    own_first = jnp.maximum(z * blocks - low_tile, 0)
    lane = x * srv + v

    def copy(src, dst, send_sem, recv_sem, target):
        return pltpu.make_async_remote_copy(
            src_ref=src, dst_ref=dst, send_sem=send_sem, recv_sem=recv_sem,
            device_id=target, device_id_type=MESH,
        )

    def send(here, src, dst, send_sem, recv_sem, target):
        @pl.when(here)
        def _():
            pltpu.make_async_copy(src, dst, recv_sem).start()

        @pl.when(jnp.logical_not(here))
        def _():
            copy(src, dst, send_sem, recv_sem, target).start()

    def sent(here, src, dst, send_sem, recv_sem, target):
        @pl.when(jnp.logical_not(here))
        def _():
            copy(src, dst, send_sem, recv_sem, target).wait_send()

    def arrived(ref, sem):
        pltpu.make_async_copy(ref, ref, sem).wait()

    barrier = pltpu.get_barrier_semaphore()

    def greet(index, carry):
        s, h, u = index // lanes, (index // srv) % heads, index % srv
        beside = (s - z == 1) | (z - s == 1)
        partner = (s == z) | ((u == v) & (beside | (h == x)))
        myself = (s == z) & (h == x) & (u == v)

        @pl.when(partner & jnp.logical_not(myself))
        def _():
            pl.semaphore_signal(barrier, inc=1, device_id=(s, h, u), device_id_type=MESH)
        return carry

    lax.fori_loop(0, dp * lanes, greet, 0)
    sides = jnp.where(z > 0, 1, 0) + jnp.where(z < dp - 1, 1, 0)
    pl.semaphore_wait(barrier, lanes - 1 + sides * heads + dp - 1 - sides)

    def key_copies(act):
        def one(index, carry):
            side, h = index // heads, index % heads
            s = z + jnp.where(side == 0, -1, jnp.where(side == 1, 1, 0))
            column = pl.ds(pl.multiple_of((h * srv + v) * HEAD_SIZE, HEAD_SIZE), HEAD_SIZE)
            start = first + home * s

            def each(c, inner):
                row = base + c * chunk - start

                @pl.when((s >= 0) & (s < dp) & (row >= 0) & (row < window))
                def _():
                    for which, ref in ((0, k_ref), (1, v_ref)):
                        act(
                            (s == z) & (h == x),
                            ref.at[pl.ds(pl.multiple_of(c * chunk, chunk), chunk), column],
                            kv_buf.at[row // TILE, which, pl.ds(pl.multiple_of(row % TILE, chunk), chunk), :],
                            kv_sem.at[index, c, which],
                            kv_got.at[row // TILE],
                            (s, h, v),
                        )
                return inner

            lax.fori_loop(0, chunks, each, 0)
            return carry

        lax.fori_loop(0, 3 * heads, one, 0)

    def doc_copies(act):
        for s in range(dp):
            act(z == s, doc_ref, docs.at[z], doc_sem.at[s], doc_got.at[z], (s, x, v))

    def query_copies(act):
        for u in range(srv):
            act(v == u, qd_ref.at[u], qd_buf.at[:, v], q_sem.at[u], q_got.at[v], (z, x, u))

    doc_copies(send)
    query_copies(send)
    key_copies(send)

    top[...] = jnp.full_like(top, NEGATIVE / 10)
    norm[...] = jnp.zeros_like(norm)
    out_t[...] = jnp.zeros_like(out_t)
    dq_t[...] = jnp.zeros_like(dq_t)
    owned[...] = jnp.zeros_like(owned)

    def contract(a, b, left, right):
        return lax.dot_general(a, b, (((left,), (right,)), ((), ())), preferred_element_type=jnp.float32)

    def turned(a):
        return a.astype(jnp.float32).T.astype(jnp.bfloat16)

    for s in range(dp):
        arrived(docs.at[s], doc_got.at[s])
    home_tile = low_tile + tiles - 1
    query_doc = docs[home_tile // blocks, pl.ds(home_tile % blocks, 1), :]
    query_doc = jnp.broadcast_to(query_doc.astype(jnp.float32), (TILE, home))
    query_at = lax.broadcasted_iota(jnp.int32, (TILE, home), 1) + home_tile * TILE
    for u in range(srv):
        arrived(qd_buf.at[:, u], q_got.at[u])
        grad_t[:, pl.ds(u * wide, wide)] = qd_buf[1, u].astype(jnp.float32).T

    def relays(act, tile):
        shard = (low_tile + tile) // blocks

        @pl.when((shard > z) & (z > 0) & (tile < tiles - 1))
        def _():
            act(copy(kv_buf.at[tile], kv_buf.at[tile + 1], relay_sem.at[tile], kv_got.at[tile + 1], (z - 1, x, v)))

        @pl.when((shard < z) & (z < dp - 1) & (tile > 0))
        def _():
            act(copy(kv_buf.at[tile], kv_buf.at[tile - 1], relay_sem.at[tile], kv_got.at[tile - 1], (z + 1, x, v)))

    def forward(i, carry):
        tile = jnp.where(i < tiles - own_first, own_first + i, tiles - 1 - i)
        index = low_tile + tile
        arrived(kv_buf.at[tile], kv_got.at[tile])
        relays(lambda c: c.start(), tile)
        key_doc = docs[index // blocks, pl.ds(index % blocks, 1), :]
        key_doc = jnp.broadcast_to(key_doc.astype(jnp.float32), (TILE, TILE)).T
        key_at = lax.broadcasted_iota(jnp.int32, (TILE, home), 0) + index * TILE
        bias = jnp.where((key_doc == query_doc) & (key_at <= query_at), 0.0, NEGATIVE)
        value_t = turned(kv_buf[tile, 1])
        keys = kv_buf[tile, 0]
        for u in range(srv):
            at = pl.ds(u * wide, wide)
            raw = contract(keys, qd_buf[0, u], 1, 1) + jnp.concatenate([bias] * pair, axis=1)
            scores[tile, :, at] = raw
            old = top[:, at]
            new = jnp.maximum(old, jnp.max(raw, axis=0, keepdims=True))
            weights = jnp.exp2((raw - new) * exponent)
            shrink = jnp.exp2((old - new) * exponent)
            top[:, at] = new
            norm[:, at] = norm[:, at] * shrink + jnp.sum(weights, axis=0, keepdims=True)
            out_t[:, at] = out_t[:, at] * shrink + contract(value_t, weights.astype(jnp.bfloat16), 1, 0)
        return carry

    lax.fori_loop(0, tiles, forward, 0)

    def att_copy(act, u):
        act(v == u, att_out.at[u], att_ref.at[v], att_sem.at[u], att_got.at[v], (z, x, u))

    def dq_copy(act, u):
        act(v == u, dq_out.at[u], dq_ref.at[v], dq_sem.at[u], dq_got.at[v], (z, x, u))

    for u in range(srv):
        at = pl.ds(u * wide, wide)
        out = (out_t[:, at] / norm[:, at]).astype(jnp.bfloat16).astype(jnp.float32)
        out_t[:, at] = out
        delta[:, at] = jnp.sum(grad_t[:, at] * out, axis=0, keepdims=True)
        top[:, at] = top[:, at] * exponent + jnp.log2(norm[:, at])

    def part_copies(act, tile):
        shard = (low_tile + tile) // blocks

        @pl.when(shard > z)
        def _():
            act(copy(part.at[tile], up_in.at[tile], part_sem.at[tile], up_got.at[tile], (z + 1, x, v)))

        @pl.when(shard < z)
        def _():
            act(copy(part.at[tile], down_in.at[tile], part_sem.at[tile], down_got.at[tile], (z - 1, x, v)))

    def grad_copies(act, least, most):
        column = pl.ds(pl.multiple_of(lane * HEAD_SIZE, HEAD_SIZE), HEAD_SIZE)

        def one(j, carry):
            @pl.when((j * piece >= least) & (j * piece < most))
            def _():
                act(
                    lane == j,
                    owned.at[:, pl.ds(pl.multiple_of(j * piece, 16), piece), :],
                    g_ref.at[:, :, column],
                    g_sem.at[j],
                    g_got.at[lane],
                    (z, j // srv, j % srv),
                )
            return carry

        lax.fori_loop(0, lanes, one, 0)

    def place(i):
        return jnp.where(i == 0, tiles - 1, jnp.where(i <= own_first, i - 1, tiles - 1 + own_first - i))

    def waits_for(tile):
        shard = (low_tile + tile) // blocks
        above = (shard >= z) & (z > 0) & (tile < tiles - 1)
        below = (shard <= z) & (z < dp - 1) & (tile > 0)
        return above, below

    def finish(tile):
        index = low_tile + tile
        shard = index // blocks

        @pl.when(shard == z)
        def _():
            row = (index - z * blocks) * TILE
            owned[:, pl.ds(pl.multiple_of(row, TILE), TILE), :] = acc[tile].astype(jnp.bfloat16)
            grad_copies(send, row, row + TILE)

        @pl.when(shard != z)
        def _():
            part[tile] = acc[tile].astype(jnp.bfloat16)
        part_copies(lambda c: c.start(), tile)

    def compute(tile):
        key_t = turned(kv_buf[tile, 0])
        values = kv_buf[tile, 1]
        key_grad = jnp.zeros((TILE, HEAD_SIZE), jnp.float32)
        value_grad = jnp.zeros((TILE, HEAD_SIZE), jnp.float32)
        for u in range(srv):
            at = pl.ds(u * wide, wide)
            probs = jnp.exp2(scores[tile, :, at] * exponent - top[:, at])
            weight_grad = contract(values, qd_buf[1, u], 1, 1)
            score_grad = (probs * (weight_grad - delta[:, at])).astype(jnp.bfloat16)
            key_grad = key_grad + contract(score_grad, qd_buf[0, u], 1, 0)
            value_grad = value_grad + contract(probs.astype(jnp.bfloat16), qd_buf[1, u], 1, 0)
            dq_t[:, at] += contract(key_t, score_grad, 1, 0)
        acc[tile, 0] = key_grad * scale
        acc[tile, 1] = value_grad

    def backward(i, carry):
        @pl.when(i < tiles)
        def _():
            tile = place(i)
            compute(tile)
            above, below = waits_for(tile)

            @pl.when(jnp.logical_not(above | below))
            def _():
                finish(tile)

        @pl.when((i >= 1) & (i <= srv))
        def _():
            u = i - 1
            att_out[u] = out_t[:, pl.ds(pl.multiple_of(u * wide, wide), wide)].T.astype(jnp.bfloat16)
            att_copy(send, u)

        @pl.when(i == tiles - 1)
        def _():
            for u in range(srv):
                dq_out[u] = (dq_t[:, pl.ds(u * wide, wide)] * scale).T.astype(jnp.bfloat16)
                dq_copy(send, u)

        @pl.when(i >= LAG)
        def _():
            tile = place(i - LAG)
            above, below = waits_for(tile)

            @pl.when(above)
            def _():
                arrived(up_in.at[tile + 1], up_got.at[tile + 1])
                acc[tile] += up_in[tile + 1].astype(jnp.float32)

            @pl.when(below)
            def _():
                arrived(down_in.at[tile - 1], down_got.at[tile - 1])
                acc[tile] += down_in[tile - 1].astype(jnp.float32)

            @pl.when(above | below)
            def _():
                finish(tile)
        return carry

    lax.fori_loop(0, tiles + LAG, backward, 0)

    extra = (z > 0) & ((low_tile - 1) // blocks == z)
    rest = jnp.minimum(jnp.maximum(low_tile - z * blocks, 0), blocks) * TILE

    @pl.when(extra)
    def _():
        arrived(up_in.at[0], up_got.at[0])
        owned[:, pl.ds(pl.multiple_of(rest - TILE, TILE), TILE), :] = up_in[0]

    grad_copies(send, 0, rest)

    doc_copies(sent)
    key_copies(sent)
    query_copies(sent)

    def settle(tile, carry):
        relays(lambda c: c.wait_send(), tile)
        part_copies(lambda c: c.wait_send(), tile)
        return carry

    lax.fori_loop(0, tiles, settle, 0)
    for u in range(srv):
        att_copy(sent, u)
        arrived(att_ref.at[u], att_got.at[u])
    for u in range(srv):
        dq_copy(sent, u)
        arrived(dq_ref.at[u], dq_got.at[u])
    grad_copies(sent, 0, blocks * TILE)
    for j in range(lanes):
        arrived(g_ref.at[:, :, pl.ds(j * HEAD_SIZE, HEAD_SIZE)], g_got.at[j])


def window_sizes(mesh_sizes, queries, keys):
    dp, heads, srv = mesh_sizes
    home, pair, width = queries.shape
    rows = keys.shape[0]
    key_total = rows * dp * heads
    longest = key_total // 2
    first = key_total - dp * home - longest
    return (dp, heads, srv, home, pair, rows, first, longest + home)


def window_fits(sizes, width):
    dp, heads, srv, home, pair, rows, first, window = sizes
    shard = rows * heads
    if width != srv * HEAD_SIZE or home != TILE or shard % TILE or first < 0 or first % TILE or window % TILE:
        return False
    if rows % srv or (rows // srv) % 16 or rows % 16:
        return False
    blocks, tiles, start = shard // TILE, window // TILE, first // TILE
    for s in range(dp):
        held = set(range(start + s, start + s + tiles))
        for other in (s - 1, s + 1):
            if 0 <= other < dp:
                for tile in range(start + other, start + other + tiles):
                    beyond = tile // blocks > s if other < s else tile // blocks < s
                    owned = tile // blocks == s
                    if (beyond or owned) and tile not in held and not (owned and other < s and tile == start + other):
                        return False
                    through = tile // blocks > s if other < s else tile // blocks < s
                    if through and tile not in held:
                        return False
    return True


def local_window(sizes, queries, keys, values, output_gradient, doc_ids):
    dp, heads, srv, home, pair, rows, first, window = sizes
    width = queries.shape[2]
    groups = width // HEAD_SIZE
    wide = pair * home
    tiles = window // TILE
    piece = rows // srv
    chunks = rows // math.gcd(TILE, rows)

    def by_group(array):
        return array.reshape(home, pair, groups, HEAD_SIZE).transpose(2, 1, 0, 3).reshape(groups, wide, HEAD_SIZE)

    both = jnp.stack([by_group(queries), by_group(output_gradient)], axis=1)
    docs = doc_ids.reshape(-1, TILE)
    vmem = pl.BlockSpec(memory_space=pltpu.VMEM)
    anywhere = pl.BlockSpec(memory_space=pl.ANY)
    outside = pl.BlockSpec(memory_space=pltpu.HBM)
    sem = pltpu.SemaphoreType.DMA
    lanes = heads * srv
    b16, f32 = jnp.bfloat16, jnp.float32
    att, dq, kv = pl.pallas_call(
        functools.partial(attend, sizes),
        out_shape=(
            jax.ShapeDtypeStruct((groups, wide, HEAD_SIZE), b16),
            jax.ShapeDtypeStruct((groups, wide, HEAD_SIZE), b16),
            jax.ShapeDtypeStruct((2, piece, lanes * HEAD_SIZE), b16),
        ),
        in_specs=[anywhere, outside, outside, outside],
        out_specs=(vmem, vmem, vmem),
        scratch_shapes=[
            pltpu.VMEM((2, srv, wide, HEAD_SIZE), b16),
            pltpu.VMEM((tiles, 2, TILE, HEAD_SIZE), b16),
            pltpu.VMEM((dp, docs.shape[0], TILE), jnp.int32),
            pltpu.VMEM((tiles, TILE, srv * wide), f32),
            pltpu.VMEM((1, srv * wide), f32),
            pltpu.VMEM((1, srv * wide), f32),
            pltpu.VMEM((1, srv * wide), f32),
            pltpu.VMEM((HEAD_SIZE, srv * wide), f32),
            pltpu.VMEM((HEAD_SIZE, srv * wide), f32),
            pltpu.VMEM((HEAD_SIZE, srv * wide), f32),
            pltpu.VMEM((tiles, 2, TILE, HEAD_SIZE), f32),
            pltpu.VMEM((tiles, 2, TILE, HEAD_SIZE), b16),
            pltpu.VMEM((tiles, 2, TILE, HEAD_SIZE), b16),
            pltpu.VMEM((tiles, 2, TILE, HEAD_SIZE), b16),
            pltpu.VMEM((2, rows * heads, HEAD_SIZE), b16),
            pltpu.VMEM((srv, wide, HEAD_SIZE), b16),
            pltpu.VMEM((srv, wide, HEAD_SIZE), b16),
            sem((srv,)), sem((srv,)),
            sem((3 * heads, chunks, 2)), sem((tiles,)), sem((tiles,)),
            sem((dp,)), sem((dp,)),
            sem((srv,)), sem((srv,)),
            sem((srv,)), sem((srv,)),
            sem((tiles,)), sem((tiles,)), sem((tiles,)),
            sem((lanes,)), sem((lanes,)),
        ],
        compiler_params=pltpu.CompilerParams(
            collective_id=0, has_side_effects=True, vmem_limit_bytes=40 * 1024 * 1024
        ),
    )(both, keys, values, docs)

    def by_row(array):
        return array.reshape(groups, pair, home, HEAD_SIZE).transpose(2, 1, 0, 3).reshape(home, pair, width)

    return by_row(att), by_row(dq), kv[0], kv[1]


def local_spread(queries, keys, values, output_gradient, doc_ids):
    home_rows, pair_heads, group_width = queries.shape
    groups = group_width // HEAD_SIZE
    scale_factor = HEAD_SIZE ** (-0.5)
    key_rows, value_rows = (
        lax.all_to_all(keys, "head", split_axis=1, concat_axis=0, tiled=True),
        lax.all_to_all(values, "head", split_axis=1, concat_axis=0, tiled=True),
    )
    key_count = key_rows.shape[0]
    servers = lax.axis_size("dp")
    server = lax.axis_index("dp")
    key_at = server * key_count + jnp.arange(key_count, dtype=jnp.int32)
    all_docs = lax.all_gather(doc_ids, "dp", axis=0, tiled=True)
    query_total = home_rows * servers
    context = all_docs.shape[0] - query_total
    query_docs = all_docs[context:]
    query_places = context + jnp.arange(query_total, dtype=jnp.int32)
    all_q, all_dout = (
        lax.all_gather(queries, "dp", axis=0, tiled=True),
        lax.all_gather(output_gradient, "dp", axis=0, tiled=True),
    )
    block_rows = math.gcd(512, query_total)
    block_count = query_total // block_rows
    key_heads = key_rows.reshape(key_count, groups, HEAD_SIZE)
    value_heads = value_rows.reshape(key_count, groups, HEAD_SIZE)
    query_blocks = all_q.reshape(block_count, block_rows, pair_heads, groups, HEAD_SIZE)
    grad_blocks = all_dout.reshape(block_count, block_rows, pair_heads, groups, HEAD_SIZE)
    place_blocks = query_places.reshape(block_count, block_rows)
    doc_blocks = query_docs.reshape(block_count, block_rows)

    def admissible(places, query_doc):
        return (key_at[None, :] <= places[:, None]) & (doc_ids[None, :] == query_doc[:, None])

    def scores_of(query_block):
        return (
            jnp.einsum("pjgd,kgd->gjpk", query_block, key_heads, preferred_element_type=jnp.float32)
            * scale_factor
        )

    def block_max(inputs):
        query_block, places, query_doc = inputs
        allowed = admissible(places, query_doc)

        def compute():
            raw_scores = scores_of(query_block)
            masked = jnp.where(allowed[None, None], raw_scores, NEGATIVE)
            return (jnp.max(masked, axis=-1).transpose(2, 1, 0), raw_scores)

        return compute()

    def block_top(inputs):
        return block_max(inputs)[0]

    local_max = lax.map(block_top, (query_blocks, place_blocks, doc_blocks))
    row_max = lax.pmax(local_max.reshape(query_total, pair_heads, groups), "dp")
    max_blocks = row_max.reshape(block_count, block_rows, pair_heads, groups)

    def block_sum(inputs):
        stored, places, query_doc, row_top = inputs
        allowed = admissible(places, query_doc)

        def compute():
            block_scores = scores_of(stored)
            shifted = block_scores - row_top.transpose(2, 1, 0)[..., None]
            weights = jnp.where(allowed[None, None], jnp.exp(shifted), 0.0)
            weighted = jnp.einsum(
                "gjpk,kgd->pjgd",
                weights.astype(jnp.bfloat16),
                value_heads,
                preferred_element_type=jnp.float32,
            )
            return (
                weighted.reshape(block_rows, pair_heads, group_width),
                jnp.sum(weights, axis=-1).transpose(2, 1, 0),
            )

        return compute()

    part_out, part_norm = lax.map(block_sum, (query_blocks, place_blocks, doc_blocks, max_blocks))
    part_out = part_out.reshape(query_total, pair_heads, group_width)
    part_norm = part_norm.reshape(query_total, pair_heads, groups)
    home_out, home_norm = (
        lax.psum_scatter(part_out, "dp", scatter_dimension=0, tiled=True),
        lax.psum_scatter(part_norm, "dp", scatter_dimension=0, tiled=True),
    )
    home_max = lax.dynamic_slice_in_dim(row_max, server * home_rows, home_rows, 0)
    attn_home = (
        home_out.reshape(home_rows, pair_heads, groups, HEAD_SIZE) / home_norm[..., None]
    ).astype(jnp.bfloat16)
    log_home = home_max + jnp.log(home_norm)
    grad_home = output_gradient.reshape(home_rows, pair_heads, groups, HEAD_SIZE).astype(
        jnp.float32
    )
    delta_home = jnp.sum(grad_home * attn_home.astype(jnp.float32), axis=-1)
    log_all, delta_all = (
        lax.all_gather(log_home, "dp", axis=0, tiled=True),
        lax.all_gather(delta_home, "dp", axis=0, tiled=True),
    )
    attention = attn_home.reshape(home_rows, pair_heads, group_width)
    log_blocks = log_all.reshape(block_count, block_rows, pair_heads, groups)
    delta_blocks = delta_all.reshape(block_count, block_rows, pair_heads, groups)

    def block_grad(totals, inputs):
        query_block, grad_block, places, query_doc, log_norm, row_delta = inputs
        allowed = admissible(places, query_doc)

        def compute():
            shifted = scores_of(query_block) - log_norm.transpose(2, 1, 0)[..., None]
            probs = jnp.where(allowed[None, None], jnp.exp(shifted), 0.0)
            value_grad = jnp.einsum(
                "gjpk,pjgd->kgd",
                probs.astype(jnp.bfloat16),
                grad_block,
                preferred_element_type=jnp.float32,
            )
            weight_grad = jnp.einsum(
                "pjgd,kgd->gjpk", grad_block, value_heads, preferred_element_type=jnp.float32
            )
            score_grad = (probs * (weight_grad - row_delta.transpose(2, 1, 0)[..., None])).astype(
                jnp.bfloat16
            )
            query_grad = (
                jnp.einsum(
                    "gjpk,kgd->pjgd", score_grad, key_heads, preferred_element_type=jnp.float32
                )
                * scale_factor
            )
            key_grad = (
                jnp.einsum(
                    "gjpk,pjgd->kgd", score_grad, query_block, preferred_element_type=jnp.float32
                )
                * scale_factor
            )
            return (query_grad.reshape(block_rows, pair_heads, group_width), key_grad, value_grad)

        query_grad, key_grad, value_grad = compute()
        return ((totals[0] + key_grad, totals[1] + value_grad), query_grad)

    zero_start = jnp.zeros((key_count, groups, HEAD_SIZE), jnp.float32)
    grad_inputs = (query_blocks, grad_blocks, place_blocks, doc_blocks, log_blocks, delta_blocks)
    (key_total, value_total), query_parts = lax.scan(
        block_grad, (zero_start, zero_start), grad_inputs
    )
    q_summed = lax.psum_scatter(
        query_parts.reshape(query_total, pair_heads, group_width).astype(jnp.bfloat16),
        "dp",
        scatter_dimension=0,
        tiled=True,
    )
    spread_key, spread_value = (
        lax.all_to_all(
            key_total.reshape(key_count, group_width).astype(jnp.bfloat16),
            "head",
            split_axis=0,
            concat_axis=1,
            tiled=True,
        ).astype(jnp.float32),
        lax.all_to_all(
            value_total.reshape(key_count, group_width).astype(jnp.bfloat16),
            "head",
            split_axis=0,
            concat_axis=1,
            tiled=True,
        ).astype(jnp.float32),
    )
    k_summed, v_summed = (
        lax.psum_scatter(
            spread_key.astype(jnp.bfloat16), "srv", scatter_dimension=0, tiled=True
        ).astype(jnp.float32),
        lax.psum_scatter(
            spread_value.astype(jnp.bfloat16), "srv", scatter_dimension=0, tiled=True
        ).astype(jnp.float32),
    )
    return (attention, q_summed, k_summed.astype(jnp.bfloat16), v_summed.astype(jnp.bfloat16))


def solution(mesh):
    placed = (
        P("dp", "srv", "head"),
        P(("dp", "head"), None),
        P(("dp", "head"), None),
        P("dp", "srv", "head"),
        P("dp"),
    )
    mesh_sizes = tuple(mesh.shape[name] for name in AXES)

    def local(queries, keys, values, output_gradient, doc_ids):
        args = (queries, keys, values, output_gradient, doc_ids)
        sizes = window_sizes(mesh_sizes, queries, keys)
        if window_fits(sizes, queries.shape[2]):
            return local_window(sizes, *args)
        return local_spread(*args)

    return jax.shard_map(
        local,
        mesh=mesh,
        in_specs=placed,
        out_specs=(
            P("dp", "srv", "head"),
            P("dp", "srv", "head"),
            P(("dp", "head", "srv"), None),
            P(("dp", "head", "srv"), None),
        ),
        check_vma=False,
    )
```

```python
import functools
import math

import jax
import jax.numpy as jnp
from jax import lax
from jax.experimental import pallas as pl
from jax.experimental.pallas import tpu as pltpu
from jax.sharding import PartitionSpec as P

HEAD_SIZE = 128


NEGATIVE = -1e30
MESH = pl.DeviceIdType.MESH
AXES = ("dp", "head", "srv")


TILE = 128
HALF = 64
LAG = 3
AHEAD = 3


def attend(sizes, q_ref, o_ref, k_ref, v_ref, doc_ref, att_ref, dq_ref, g_ref,
           raw, stage, qd_buf, kv_buf, docs, scores, top, norm, delta, out_t, grad_t, dq_t, acc, part, up_in, down_in, owned, att_out, dq_out,
           raw_got, q_sem, q_got, kv_sem, kv_got, relay_sem, doc_sem, doc_got, att_sem, att_got, dq_sem, dq_got,
           part_sem, up_got, down_got, g_sem, g_got):
    dp, heads, srv, home, pair, rows, first, window = sizes
    piece = rows // srv
    wide = pair * home
    every = srv * wide
    tiles = window // TILE
    blocks = rows * heads // TILE
    lanes = heads * srv
    scale = HEAD_SIZE ** (-0.5)
    exponent = scale * math.log2(math.e)
    z, x, v = (lax.axis_index(name) for name in AXES)
    base = (z * heads + x) * rows
    low = first + home * z
    low_tile = low // TILE
    own_first = jnp.maximum(z * blocks - low_tile, 0)
    lane = x * srv + v

    def copy(src, dst, send_sem, recv_sem, target):
        return pltpu.make_async_remote_copy(
            src_ref=src, dst_ref=dst, send_sem=send_sem, recv_sem=recv_sem,
            device_id=target, device_id_type=MESH,
        )

    def send(here, src, dst, send_sem, recv_sem, target):
        @pl.when(here)
        def _():
            pltpu.make_async_copy(src, dst, recv_sem).start()

        @pl.when(jnp.logical_not(here))
        def _():
            copy(src, dst, send_sem, recv_sem, target).start()

    def sent(here, src, dst, send_sem, recv_sem, target):
        @pl.when(jnp.logical_not(here))
        def _():
            copy(src, dst, send_sem, recv_sem, target).wait_send()

    def arrived(ref, sem):
        pltpu.make_async_copy(ref, ref, sem).wait()

    for which, ref in ((0, q_ref), (1, o_ref)):
        pltpu.make_async_copy(ref, raw.at[which], raw_got.at[which]).start()

    def stage_queries():
        for which in range(2):
            arrived(raw.at[which], raw_got.at[which])
            for u in range(srv):
                block = raw[which, :, :, pl.ds(u * HEAD_SIZE, HEAD_SIZE)].astype(jnp.float32)
                for j in range(pair):
                    stage[u, which, pl.ds(j * home, home), :] = block[:, j, :].astype(jnp.bfloat16)

    barrier = pltpu.get_barrier_semaphore()

    def greet(index, carry):
        s, h, u = index // lanes, (index // srv) % heads, index % srv
        beside = (s - z == 1) | (z - s == 1)
        partner = (s == z) | ((u == v) & (beside | (h == x)))
        myself = (s == z) & (h == x) & (u == v)

        @pl.when(partner & jnp.logical_not(myself))
        def _():
            pl.semaphore_signal(barrier, inc=1, device_id=(s, h, u), device_id_type=MESH)
        return carry

    lax.fori_loop(0, dp * lanes, greet, 0)
    sides = jnp.where(z > 0, 1, 0) + jnp.where(z < dp - 1, 1, 0)
    pl.semaphore_wait(barrier, lanes - 1 + sides * heads + dp - 1 - sides)

    def key_copies(act):
        def one(index, carry):
            side, h = index // heads, (x + index) % heads
            s = z + side - 1
            column = pl.ds(pl.multiple_of((h * srv + v) * HEAD_SIZE, HEAD_SIZE), HEAD_SIZE)
            start = first + home * s

            def each(at, count, slot):
                row = base + at - start

                @pl.when((s >= 0) & (s < dp) & (row >= 0) & (row < window))
                def _():
                    for which, ref in ((0, k_ref), (1, v_ref)):
                        act(
                            (s == z) & (h == x),
                            ref.at[pl.ds(pl.multiple_of(at, HALF), count), column],
                            kv_buf.at[row // TILE, which, pl.ds(pl.multiple_of(row % TILE, count), count), :],
                            kv_sem.at[index, slot, which],
                            kv_got.at[row // TILE],
                            (s, h, v),
                        )

            for c in range(rows // TILE):
                each(c * TILE + base % TILE, TILE, c)
            if rows % TILE:
                each(jnp.where(base % TILE == 0, rows - HALF, 0), HALF, rows // TILE)
            return carry

        lax.fori_loop(0, 3 * heads, one, 0)

    def doc_copies(act):
        for s in range(dp):
            act(z == s, doc_ref, docs.at[z], doc_sem.at[s], doc_got.at[z], (s, x, v))

    def query_copies(act):
        for u in range(srv):
            act(v == u, stage.at[u], qd_buf.at[:, v], q_sem.at[u], q_got.at[v], (z, x, u))

    key_copies(send)
    doc_copies(send)
    stage_queries()
    query_copies(send)

    top[...] = jnp.full_like(top, NEGATIVE / 10)
    norm[...] = jnp.zeros_like(norm)
    out_t[...] = jnp.zeros_like(out_t)
    dq_t[...] = jnp.zeros_like(dq_t)
    owned[...] = jnp.zeros_like(owned)

    def contract(a, b, left, right):
        return lax.dot_general(a, b, (((left,), (right,)), ((), ())), preferred_element_type=jnp.float32)

    def turned(a):
        return a.astype(jnp.float32).T.astype(jnp.bfloat16)

    for s in range(dp):
        arrived(docs.at[s], doc_got.at[s])
    home_tile = low_tile + tiles - 1
    query_doc = docs[home_tile // blocks, pl.ds(home_tile % blocks, 1), :]
    query_doc = jnp.broadcast_to(query_doc.astype(jnp.float32), (TILE, home))
    query_at = lax.broadcasted_iota(jnp.int32, (TILE, home), 1) + home_tile * TILE
    for u in range(srv):
        arrived(qd_buf.at[:, u], q_got.at[u])
        grad_t[:, pl.ds(u * wide, wide)] = qd_buf[1, u].astype(jnp.float32).T

    def relays(act, tile):
        shard = (low_tile + tile) // blocks

        @pl.when((shard > z) & (z > 0) & (tile < tiles - 1))
        def _():
            act(copy(kv_buf.at[tile], kv_buf.at[tile + 1], relay_sem.at[tile], kv_got.at[tile + 1], (z - 1, x, v)))

        @pl.when((shard < z) & (z < dp - 1) & (tile > 0))
        def _():
            act(copy(kv_buf.at[tile], kv_buf.at[tile - 1], relay_sem.at[tile], kv_got.at[tile - 1], (z + 1, x, v)))

    ahead = jnp.where((z > 0) & (z < dp - 1), AHEAD, 0)

    def forward(i, carry):
        def turn(i):
            return jnp.where(i < tiles - own_first, own_first + i, tiles - 1 - i)

        @pl.when(i < tiles)
        def _():
            tile = turn(i)
            arrived(kv_buf.at[tile], kv_got.at[tile])
            relays(lambda c: c.start(), tile)

        @pl.when((i >= ahead) & (i < tiles + ahead))
        def _():
            meet(turn(i - ahead))
        return carry

    def meet(tile):
        index = low_tile + tile
        key_doc = docs[index // blocks, pl.ds(index % blocks, 1), :]
        key_doc = jnp.broadcast_to(key_doc.astype(jnp.float32), (TILE, TILE)).T
        key_at = lax.broadcasted_iota(jnp.int32, (TILE, home), 0) + index * TILE
        bias = jnp.where((key_doc == query_doc) & (key_at <= query_at), 0.0, NEGATIVE)
        value_t = turned(kv_buf[tile, 1])
        keys = kv_buf[tile, 0]
        for u in range(srv):
            at = pl.ds(u * wide, wide)
            raw = contract(keys, qd_buf[0, u], 1, 1) + jnp.concatenate([bias] * pair, axis=1)
            scores[tile, :, at] = raw
            old = top[:, at]
            new = jnp.maximum(old, jnp.max(raw, axis=0, keepdims=True))
            weights = jnp.exp2((raw - new) * exponent)
            shrink = jnp.exp2((old - new) * exponent)
            top[:, at] = new
            norm[:, at] = norm[:, at] * shrink + jnp.sum(weights, axis=0, keepdims=True)
            out_t[:, at] = out_t[:, at] * shrink + contract(value_t, weights.astype(jnp.bfloat16), 1, 0)

    lax.fori_loop(0, tiles + AHEAD, forward, 0)

    def att_copy(act, u):
        act(v == u, att_out.at[u], att_ref.at[v], att_sem.at[u], att_got.at[v], (z, x, u))

    def dq_copy(act, u):
        act(v == u, dq_out.at[u], dq_ref.at[v], dq_sem.at[u], dq_got.at[v], (z, x, u))

    for u in range(srv):
        at = pl.ds(u * wide, wide)
        out = (out_t[:, at] / norm[:, at]).astype(jnp.bfloat16).astype(jnp.float32)
        out_t[:, at] = out
        delta[:, at] = jnp.sum(grad_t[:, at] * out, axis=0, keepdims=True)
        top[:, at] = top[:, at] * exponent + jnp.log2(norm[:, at])

    def part_copies(act, tile):
        shard = (low_tile + tile) // blocks

        @pl.when(shard > z)
        def _():
            act(copy(part.at[tile], up_in.at[tile], part_sem.at[tile], up_got.at[tile], (z + 1, x, v)))

        @pl.when(shard < z)
        def _():
            act(copy(part.at[tile], down_in.at[tile], part_sem.at[tile], down_got.at[tile], (z - 1, x, v)))

    def grad_copies(act, least, most):
        column = pl.ds(pl.multiple_of(lane * HEAD_SIZE, HEAD_SIZE), HEAD_SIZE)

        def one(j, carry):
            @pl.when((j * piece >= least) & (j * piece < most))
            def _():
                act(
                    lane == j,
                    owned.at[:, pl.ds(pl.multiple_of(j * piece, 16), piece), :],
                    g_ref.at[:, :, column],
                    g_sem.at[j],
                    g_got.at[lane],
                    (z, j // srv, j % srv),
                )
            return carry

        lax.fori_loop(0, lanes, one, 0)

    def place(i):
        return jnp.where(i == 0, tiles - 1, jnp.where(i <= own_first, i - 1, tiles - 1 + own_first - i))

    def waits_for(tile):
        shard = (low_tile + tile) // blocks
        above = (shard >= z) & (z > 0) & (tile < tiles - 1)
        below = (shard <= z) & (z < dp - 1) & (tile > 0)
        return above, below

    def finish(tile):
        index = low_tile + tile
        shard = index // blocks

        @pl.when(shard == z)
        def _():
            row = (index - z * blocks) * TILE
            owned[:, pl.ds(pl.multiple_of(row, TILE), TILE), :] = acc[tile].astype(jnp.bfloat16)
            grad_copies(send, row, row + TILE)

        @pl.when(shard != z)
        def _():
            part[tile] = acc[tile].astype(jnp.bfloat16)
        part_copies(lambda c: c.start(), tile)

    def compute(tile):
        key_t = turned(kv_buf[tile, 0])
        values = kv_buf[tile, 1]
        key_grad = jnp.zeros((TILE, HEAD_SIZE), jnp.float32)
        value_grad = jnp.zeros((TILE, HEAD_SIZE), jnp.float32)
        for u in range(srv):
            at = pl.ds(u * wide, wide)
            probs = jnp.exp2(scores[tile, :, at] * exponent - top[:, at])
            weight_grad = contract(values, qd_buf[1, u], 1, 1)
            score_grad = (probs * (weight_grad - delta[:, at])).astype(jnp.bfloat16)
            key_grad = key_grad + contract(score_grad, qd_buf[0, u], 1, 0)
            value_grad = value_grad + contract(probs.astype(jnp.bfloat16), qd_buf[1, u], 1, 0)
            dq_t[:, at] += contract(key_t, score_grad, 1, 0)
        acc[tile, 0] = key_grad * scale
        acc[tile, 1] = value_grad

    def backward(i, carry):
        @pl.when(i < tiles)
        def _():
            tile = place(i)
            compute(tile)
            above, below = waits_for(tile)

            @pl.when(jnp.logical_not(above | below))
            def _():
                finish(tile)

        @pl.when((i >= 1) & (i <= srv))
        def _():
            u = i - 1
            att_out[u] = out_t[:, pl.ds(pl.multiple_of(u * wide, wide), wide)].T.astype(jnp.bfloat16)
            att_copy(send, u)

        @pl.when(i == tiles - 1)
        def _():
            for u in range(srv):
                dq_out[u] = (dq_t[:, pl.ds(u * wide, wide)] * scale).T.astype(jnp.bfloat16)
                dq_copy(send, u)

        @pl.when(i >= LAG)
        def _():
            tile = place(i - LAG)
            above, below = waits_for(tile)

            @pl.when(above)
            def _():
                arrived(up_in.at[tile + 1], up_got.at[tile + 1])
                acc[tile] += up_in[tile + 1].astype(jnp.float32)

            @pl.when(below)
            def _():
                arrived(down_in.at[tile - 1], down_got.at[tile - 1])
                acc[tile] += down_in[tile - 1].astype(jnp.float32)

            @pl.when(above | below)
            def _():
                finish(tile)
        return carry

    extra = (z > 0) & ((low_tile - 1) // blocks == z)
    rest = jnp.minimum(jnp.maximum(low_tile - z * blocks, 0), blocks) * TILE
    idle = jnp.where(extra, jnp.maximum(rest - TILE - piece + 1, 0), rest)
    grad_copies(send, 0, idle)
    lax.fori_loop(0, tiles + LAG, backward, 0)

    @pl.when(extra)
    def _():
        arrived(up_in.at[0], up_got.at[0])
        owned[:, pl.ds(pl.multiple_of(rest - TILE, TILE), TILE), :] = up_in[0]

    grad_copies(send, idle, rest)

    doc_copies(sent)
    key_copies(sent)
    query_copies(sent)

    def settle(tile, carry):
        relays(lambda c: c.wait_send(), tile)
        part_copies(lambda c: c.wait_send(), tile)
        return carry

    lax.fori_loop(0, tiles, settle, 0)
    for u in range(srv):
        att_copy(sent, u)
        arrived(att_ref.at[u], att_got.at[u])
    for u in range(srv):
        dq_copy(sent, u)
        arrived(dq_ref.at[u], dq_got.at[u])
    grad_copies(sent, 0, blocks * TILE)
    for j in range(lanes):
        arrived(g_ref.at[:, :, pl.ds(j * HEAD_SIZE, HEAD_SIZE)], g_got.at[j])


def window_sizes(mesh_sizes, queries, keys):
    dp, heads, srv = mesh_sizes
    home, pair, width = queries.shape
    rows = keys.shape[0]
    key_total = rows * dp * heads
    longest = key_total // 2
    first = key_total - dp * home - longest
    return (dp, heads, srv, home, pair, rows, first, longest + home)


def window_fits(sizes, width):
    dp, heads, srv, home, pair, rows, first, window = sizes
    shard = rows * heads
    if width != srv * HEAD_SIZE or home != TILE or shard % TILE or first < 0 or first % TILE or window % TILE:
        return False
    if rows % HALF or rows % srv or (rows // srv) % 16 or rows % 16:
        return False
    blocks, tiles, start = shard // TILE, window // TILE, first // TILE
    for s in range(dp):
        held = set(range(start + s, start + s + tiles))
        for other in (s - 1, s + 1):
            if 0 <= other < dp:
                for tile in range(start + other, start + other + tiles):
                    beyond = tile // blocks > s if other < s else tile // blocks < s
                    owned = tile // blocks == s
                    if (beyond or owned) and tile not in held and not (owned and other < s and tile == start + other):
                        return False
                    through = tile // blocks > s if other < s else tile // blocks < s
                    if through and tile not in held:
                        return False
    return True


def local_window(sizes, queries, keys, values, output_gradient, doc_ids):
    dp, heads, srv, home, pair, rows, first, window = sizes
    width = queries.shape[2]
    groups = width // HEAD_SIZE
    wide = pair * home
    tiles = window // TILE
    piece = rows // srv
    chunks = -(-rows // TILE)

    docs = doc_ids.reshape(-1, TILE)
    vmem = pl.BlockSpec(memory_space=pltpu.VMEM)
    outside = pl.BlockSpec(memory_space=pltpu.HBM)
    sem = pltpu.SemaphoreType.DMA
    lanes = heads * srv
    b16, f32 = jnp.bfloat16, jnp.float32
    att, dq, kv = pl.pallas_call(
        functools.partial(attend, sizes),
        out_shape=(
            jax.ShapeDtypeStruct((groups, wide, HEAD_SIZE), b16),
            jax.ShapeDtypeStruct((groups, wide, HEAD_SIZE), b16),
            jax.ShapeDtypeStruct((2, piece, lanes * HEAD_SIZE), b16),
        ),
        in_specs=[outside] * 5,
        out_specs=(vmem, vmem, vmem),
        scratch_shapes=[
            pltpu.VMEM((2, home, pair, width), b16),
            pltpu.VMEM((srv, 2, wide, HEAD_SIZE), b16),
            pltpu.VMEM((2, srv, wide, HEAD_SIZE), b16),
            pltpu.VMEM((tiles, 2, TILE, HEAD_SIZE), b16),
            pltpu.VMEM((dp, docs.shape[0], TILE), jnp.int32),
            pltpu.VMEM((tiles, TILE, srv * wide), f32),
            pltpu.VMEM((1, srv * wide), f32),
            pltpu.VMEM((1, srv * wide), f32),
            pltpu.VMEM((1, srv * wide), f32),
            pltpu.VMEM((HEAD_SIZE, srv * wide), f32),
            pltpu.VMEM((HEAD_SIZE, srv * wide), f32),
            pltpu.VMEM((HEAD_SIZE, srv * wide), f32),
            pltpu.VMEM((tiles, 2, TILE, HEAD_SIZE), f32),
            pltpu.VMEM((tiles, 2, TILE, HEAD_SIZE), b16),
            pltpu.VMEM((tiles, 2, TILE, HEAD_SIZE), b16),
            pltpu.VMEM((tiles, 2, TILE, HEAD_SIZE), b16),
            pltpu.VMEM((2, rows * heads, HEAD_SIZE), b16),
            pltpu.VMEM((srv, wide, HEAD_SIZE), b16),
            pltpu.VMEM((srv, wide, HEAD_SIZE), b16),
            sem((2,)), sem((srv,)), sem((srv,)),
            sem((3 * heads, chunks, 2)), sem((tiles,)), sem((tiles,)),
            sem((dp,)), sem((dp,)),
            sem((srv,)), sem((srv,)),
            sem((srv,)), sem((srv,)),
            sem((tiles,)), sem((tiles,)), sem((tiles,)),
            sem((lanes,)), sem((lanes,)),
        ],
        compiler_params=pltpu.CompilerParams(
            collective_id=0, has_side_effects=True, vmem_limit_bytes=63 * 1024 * 1024
        ),
    )(queries, output_gradient, keys, values, docs)

    def by_row(array):
        return array.reshape(groups, pair, home, HEAD_SIZE).transpose(2, 1, 0, 3).reshape(home, pair, width)

    return by_row(att), by_row(dq), kv[0], kv[1]


def local_spread(queries, keys, values, output_gradient, doc_ids):
    home_rows, pair_heads, group_width = queries.shape
    groups = group_width // HEAD_SIZE
    scale_factor = HEAD_SIZE ** (-0.5)
    key_rows, value_rows = (
        lax.all_to_all(keys, "head", split_axis=1, concat_axis=0, tiled=True),
        lax.all_to_all(values, "head", split_axis=1, concat_axis=0, tiled=True),
    )
    key_count = key_rows.shape[0]
    servers = lax.axis_size("dp")
    server = lax.axis_index("dp")
    key_at = server * key_count + jnp.arange(key_count, dtype=jnp.int32)
    all_docs = lax.all_gather(doc_ids, "dp", axis=0, tiled=True)
    query_total = home_rows * servers
    context = all_docs.shape[0] - query_total
    query_docs = all_docs[context:]
    query_places = context + jnp.arange(query_total, dtype=jnp.int32)
    all_q, all_dout = (
        lax.all_gather(queries, "dp", axis=0, tiled=True),
        lax.all_gather(output_gradient, "dp", axis=0, tiled=True),
    )
    block_rows = math.gcd(512, query_total)
    block_count = query_total // block_rows
    key_heads = key_rows.reshape(key_count, groups, HEAD_SIZE)
    value_heads = value_rows.reshape(key_count, groups, HEAD_SIZE)
    query_blocks = all_q.reshape(block_count, block_rows, pair_heads, groups, HEAD_SIZE)
    grad_blocks = all_dout.reshape(block_count, block_rows, pair_heads, groups, HEAD_SIZE)
    place_blocks = query_places.reshape(block_count, block_rows)
    doc_blocks = query_docs.reshape(block_count, block_rows)

    def admissible(places, query_doc):
        return (key_at[None, :] <= places[:, None]) & (doc_ids[None, :] == query_doc[:, None])

    def scores_of(query_block):
        return (
            jnp.einsum("pjgd,kgd->gjpk", query_block, key_heads, preferred_element_type=jnp.float32)
            * scale_factor
        )

    def block_max(inputs):
        query_block, places, query_doc = inputs
        allowed = admissible(places, query_doc)

        def compute():
            raw_scores = scores_of(query_block)
            masked = jnp.where(allowed[None, None], raw_scores, NEGATIVE)
            return (jnp.max(masked, axis=-1).transpose(2, 1, 0), raw_scores)

        return compute()

    def block_top(inputs):
        return block_max(inputs)[0]

    local_max = lax.map(block_top, (query_blocks, place_blocks, doc_blocks))
    row_max = lax.pmax(local_max.reshape(query_total, pair_heads, groups), "dp")
    max_blocks = row_max.reshape(block_count, block_rows, pair_heads, groups)

    def block_sum(inputs):
        stored, places, query_doc, row_top = inputs
        allowed = admissible(places, query_doc)

        def compute():
            block_scores = scores_of(stored)
            shifted = block_scores - row_top.transpose(2, 1, 0)[..., None]
            weights = jnp.where(allowed[None, None], jnp.exp(shifted), 0.0)
            weighted = jnp.einsum(
                "gjpk,kgd->pjgd",
                weights.astype(jnp.bfloat16),
                value_heads,
                preferred_element_type=jnp.float32,
            )
            return (
                weighted.reshape(block_rows, pair_heads, group_width),
                jnp.sum(weights, axis=-1).transpose(2, 1, 0),
            )

        return compute()

    part_out, part_norm = lax.map(block_sum, (query_blocks, place_blocks, doc_blocks, max_blocks))
    part_out = part_out.reshape(query_total, pair_heads, group_width)
    part_norm = part_norm.reshape(query_total, pair_heads, groups)
    home_out, home_norm = (
        lax.psum_scatter(part_out, "dp", scatter_dimension=0, tiled=True),
        lax.psum_scatter(part_norm, "dp", scatter_dimension=0, tiled=True),
    )
    home_max = lax.dynamic_slice_in_dim(row_max, server * home_rows, home_rows, 0)
    attn_home = (
        home_out.reshape(home_rows, pair_heads, groups, HEAD_SIZE) / home_norm[..., None]
    ).astype(jnp.bfloat16)
    log_home = home_max + jnp.log(home_norm)
    grad_home = output_gradient.reshape(home_rows, pair_heads, groups, HEAD_SIZE).astype(
        jnp.float32
    )
    delta_home = jnp.sum(grad_home * attn_home.astype(jnp.float32), axis=-1)
    log_all, delta_all = (
        lax.all_gather(log_home, "dp", axis=0, tiled=True),
        lax.all_gather(delta_home, "dp", axis=0, tiled=True),
    )
    attention = attn_home.reshape(home_rows, pair_heads, group_width)
    log_blocks = log_all.reshape(block_count, block_rows, pair_heads, groups)
    delta_blocks = delta_all.reshape(block_count, block_rows, pair_heads, groups)

    def block_grad(totals, inputs):
        query_block, grad_block, places, query_doc, log_norm, row_delta = inputs
        allowed = admissible(places, query_doc)

        def compute():
            shifted = scores_of(query_block) - log_norm.transpose(2, 1, 0)[..., None]
            probs = jnp.where(allowed[None, None], jnp.exp(shifted), 0.0)
            value_grad = jnp.einsum(
                "gjpk,pjgd->kgd",
                probs.astype(jnp.bfloat16),
                grad_block,
                preferred_element_type=jnp.float32,
            )
            weight_grad = jnp.einsum(
                "pjgd,kgd->gjpk", grad_block, value_heads, preferred_element_type=jnp.float32
            )
            score_grad = (probs * (weight_grad - row_delta.transpose(2, 1, 0)[..., None])).astype(
                jnp.bfloat16
            )
            query_grad = (
                jnp.einsum(
                    "gjpk,kgd->pjgd", score_grad, key_heads, preferred_element_type=jnp.float32
                )
                * scale_factor
            )
            key_grad = (
                jnp.einsum(
                    "gjpk,pjgd->kgd", score_grad, query_block, preferred_element_type=jnp.float32
                )
                * scale_factor
            )
            return (query_grad.reshape(block_rows, pair_heads, group_width), key_grad, value_grad)

        query_grad, key_grad, value_grad = compute()
        return ((totals[0] + key_grad, totals[1] + value_grad), query_grad)

    zero_start = jnp.zeros((key_count, groups, HEAD_SIZE), jnp.float32)
    grad_inputs = (query_blocks, grad_blocks, place_blocks, doc_blocks, log_blocks, delta_blocks)
    (key_total, value_total), query_parts = lax.scan(
        block_grad, (zero_start, zero_start), grad_inputs
    )
    q_summed = lax.psum_scatter(
        query_parts.reshape(query_total, pair_heads, group_width).astype(jnp.bfloat16),
        "dp",
        scatter_dimension=0,
        tiled=True,
    )
    spread_key, spread_value = (
        lax.all_to_all(
            key_total.reshape(key_count, group_width).astype(jnp.bfloat16),
            "head",
            split_axis=0,
            concat_axis=1,
            tiled=True,
        ).astype(jnp.float32),
        lax.all_to_all(
            value_total.reshape(key_count, group_width).astype(jnp.bfloat16),
            "head",
            split_axis=0,
            concat_axis=1,
            tiled=True,
        ).astype(jnp.float32),
    )
    k_summed, v_summed = (
        lax.psum_scatter(
            spread_key.astype(jnp.bfloat16), "srv", scatter_dimension=0, tiled=True
        ).astype(jnp.float32),
        lax.psum_scatter(
            spread_value.astype(jnp.bfloat16), "srv", scatter_dimension=0, tiled=True
        ).astype(jnp.float32),
    )
    return (attention, q_summed, k_summed.astype(jnp.bfloat16), v_summed.astype(jnp.bfloat16))


def solution(mesh):
    placed = (
        P("dp", "srv", "head"),
        P(("dp", "head"), None),
        P(("dp", "head"), None),
        P("dp", "srv", "head"),
        P("dp"),
    )
    mesh_sizes = tuple(mesh.shape[name] for name in AXES)

    def local(queries, keys, values, output_gradient, doc_ids):
        args = (queries, keys, values, output_gradient, doc_ids)
        sizes = window_sizes(mesh_sizes, queries, keys)
        if window_fits(sizes, queries.shape[2]):
            return local_window(sizes, *args)
        return local_spread(*args)

    return jax.shard_map(
        local,
        mesh=mesh,
        in_specs=placed,
        out_specs=(
            P("dp", "srv", "head"),
            P("dp", "srv", "head"),
            P(("dp", "head", "srv"), None),
            P(("dp", "head", "srv"), None),
        ),
        check_vma=False,
    )
```

```python
import functools
import math

import jax
import jax.numpy as jnp
from jax import lax
from jax.experimental import pallas as pl
from jax.experimental.pallas import tpu as pltpu
from jax.sharding import PartitionSpec as P

HEAD_SIZE = 128


NEGATIVE = -1e30
MESH = pl.DeviceIdType.MESH
AXES = ("dp", "head", "srv")


TILE = 128
HALF = 64
LAG = 3
AHEAD = 3


def attend(sizes, q_ref, o_ref, k_ref, v_ref, doc_ref, att_ref, dq_ref, g_ref,
           raw, stage, qd_buf, kv_buf, docs, scores, top, norm, delta, out_t, grad_t, dq_t, acc, part, up_in, down_in, owned, att_out, dq_out, att_in, dq_in,
           raw_got, q_sem, q_got, kv_sem, kv_got, relay_sem, doc_sem, doc_got, att_sem, att_got, dq_sem, dq_got,
           part_sem, up_got, down_got, g_sem, g_got):
    dp, heads, srv, home, pair, rows, first, window = sizes
    piece = rows // srv
    wide = pair * home
    every = srv * wide
    tiles = window // TILE
    blocks = rows * heads // TILE
    lanes = heads * srv
    scale = HEAD_SIZE ** (-0.5)
    exponent = scale * math.log2(math.e)
    z, x, v = (lax.axis_index(name) for name in AXES)
    base = (z * heads + x) * rows
    low = first + home * z
    low_tile = low // TILE
    own_first = jnp.maximum(z * blocks - low_tile, 0)
    lane = x * srv + v

    def copy(src, dst, send_sem, recv_sem, target):
        return pltpu.make_async_remote_copy(
            src_ref=src, dst_ref=dst, send_sem=send_sem, recv_sem=recv_sem,
            device_id=target, device_id_type=MESH,
        )

    def send(here, src, dst, send_sem, recv_sem, target):
        @pl.when(here)
        def _():
            pltpu.make_async_copy(src, dst, recv_sem).start()

        @pl.when(jnp.logical_not(here))
        def _():
            copy(src, dst, send_sem, recv_sem, target).start()

    def sent(here, src, dst, send_sem, recv_sem, target):
        @pl.when(jnp.logical_not(here))
        def _():
            copy(src, dst, send_sem, recv_sem, target).wait_send()

    def arrived(ref, sem):
        pltpu.make_async_copy(ref, ref, sem).wait()

    for which, ref in ((0, q_ref), (1, o_ref)):
        pltpu.make_async_copy(ref, raw.at[which], raw_got.at[which]).start()

    def stage_queries():
        for which in range(2):
            arrived(raw.at[which], raw_got.at[which])
            for u in range(srv):
                block = raw[which, :, :, pl.ds(u * HEAD_SIZE, HEAD_SIZE)].astype(jnp.float32)
                for j in range(pair):
                    stage[u, which, pl.ds(j * home, home), :] = block[:, j, :].astype(jnp.bfloat16)

    def by_row(source, target, u):
        heads_of = [source[u, pl.ds(j * home, home), :].astype(jnp.float32) for j in range(pair)]
        target[:, :, pl.ds(u * HEAD_SIZE, HEAD_SIZE)] = jnp.stack(heads_of, axis=1).astype(jnp.bfloat16)

    barrier = pltpu.get_barrier_semaphore()

    def greet(index, carry):
        s, h, u = index // lanes, (index // srv) % heads, index % srv
        beside = (s - z == 1) | (z - s == 1)
        partner = (s == z) | ((u == v) & (beside | (h == x)))
        myself = (s == z) & (h == x) & (u == v)

        @pl.when(partner & jnp.logical_not(myself))
        def _():
            pl.semaphore_signal(barrier, inc=1, device_id=(s, h, u), device_id_type=MESH)
        return carry

    lax.fori_loop(0, dp * lanes, greet, 0)
    sides = jnp.where(z > 0, 1, 0) + jnp.where(z < dp - 1, 1, 0)
    pl.semaphore_wait(barrier, lanes - 1 + sides * heads + dp - 1 - sides)

    def key_copies(act):
        def one(index, carry):
            side, h = index // heads, (x + index) % heads
            s = z + side - 1
            column = pl.ds(pl.multiple_of((h * srv + v) * HEAD_SIZE, HEAD_SIZE), HEAD_SIZE)
            start = first + home * s

            def each(at, count, slot):
                row = base + at - start

                @pl.when((s >= 0) & (s < dp) & (row >= 0) & (row < window))
                def _():
                    for which, ref in ((0, k_ref), (1, v_ref)):
                        act(
                            (s == z) & (h == x),
                            ref.at[pl.ds(pl.multiple_of(at, HALF), count), column],
                            kv_buf.at[row // TILE, which, pl.ds(pl.multiple_of(row % TILE, count), count), :],
                            kv_sem.at[index, slot, which],
                            kv_got.at[row // TILE],
                            (s, h, v),
                        )

            for c in range(rows // TILE):
                each(c * TILE + base % TILE, TILE, c)
            if rows % TILE:
                each(jnp.where(base % TILE == 0, rows - HALF, 0), HALF, rows // TILE)
            return carry

        lax.fori_loop(0, 3 * heads, one, 0)

    def doc_copies(act):
        for s in range(dp):
            act(z == s, doc_ref, docs.at[z], doc_sem.at[s], doc_got.at[z], (s, x, v))

    def query_copies(act):
        for u in range(srv):
            act(v == u, stage.at[u], qd_buf.at[:, v], q_sem.at[u], q_got.at[v], (z, x, u))

    key_copies(send)
    doc_copies(send)
    stage_queries()
    query_copies(send)

    top[...] = jnp.full_like(top, NEGATIVE / 10)
    norm[...] = jnp.zeros_like(norm)
    out_t[...] = jnp.zeros_like(out_t)
    dq_t[...] = jnp.zeros_like(dq_t)
    owned[...] = jnp.zeros_like(owned)

    def contract(a, b, left, right):
        return lax.dot_general(a, b, (((left,), (right,)), ((), ())), preferred_element_type=jnp.float32)

    def turned(a):
        return a.astype(jnp.float32).T.astype(jnp.bfloat16)

    for s in range(dp):
        arrived(docs.at[s], doc_got.at[s])
    home_tile = low_tile + tiles - 1
    query_doc = docs[home_tile // blocks, pl.ds(home_tile % blocks, 1), :]
    query_doc = jnp.broadcast_to(query_doc.astype(jnp.float32), (TILE, home))
    query_at = lax.broadcasted_iota(jnp.int32, (TILE, home), 1) + home_tile * TILE
    for u in range(srv):
        arrived(qd_buf.at[:, u], q_got.at[u])
        grad_t[:, pl.ds(u * wide, wide)] = qd_buf[1, u].astype(jnp.float32).T

    def relays(act, tile):
        shard = (low_tile + tile) // blocks

        @pl.when((shard > z) & (z > 0) & (tile < tiles - 1))
        def _():
            act(copy(kv_buf.at[tile], kv_buf.at[tile + 1], relay_sem.at[tile], kv_got.at[tile + 1], (z - 1, x, v)))

        @pl.when((shard < z) & (z < dp - 1) & (tile > 0))
        def _():
            act(copy(kv_buf.at[tile], kv_buf.at[tile - 1], relay_sem.at[tile], kv_got.at[tile - 1], (z + 1, x, v)))

    ahead = jnp.where((z > 0) & (z < dp - 1), AHEAD, 0)

    def forward(i, carry):
        def turn(i):
            return jnp.where(i < tiles - own_first, own_first + i, tiles - 1 - i)

        @pl.when(i < tiles)
        def _():
            tile = turn(i)
            arrived(kv_buf.at[tile], kv_got.at[tile])
            relays(lambda c: c.start(), tile)

        @pl.when((i >= ahead) & (i < tiles + ahead))
        def _():
            meet(turn(i - ahead))
        return carry

    def meet(tile):
        index = low_tile + tile
        key_doc = docs[index // blocks, pl.ds(index % blocks, 1), :]
        key_doc = jnp.broadcast_to(key_doc.astype(jnp.float32), (TILE, TILE)).T
        key_at = lax.broadcasted_iota(jnp.int32, (TILE, home), 0) + index * TILE
        bias = jnp.where((key_doc == query_doc) & (key_at <= query_at), 0.0, NEGATIVE)
        value_t = turned(kv_buf[tile, 1])
        keys = kv_buf[tile, 0]
        for u in range(srv):
            at = pl.ds(u * wide, wide)
            raw = contract(keys, qd_buf[0, u], 1, 1) + jnp.concatenate([bias] * pair, axis=1)
            scores[tile, :, at] = raw
            old = top[:, at]
            new = jnp.maximum(old, jnp.max(raw, axis=0, keepdims=True))
            weights = jnp.exp2((raw - new) * exponent)
            shrink = jnp.exp2((old - new) * exponent)
            top[:, at] = new
            norm[:, at] = norm[:, at] * shrink + jnp.sum(weights, axis=0, keepdims=True)
            out_t[:, at] = out_t[:, at] * shrink + contract(value_t, weights.astype(jnp.bfloat16), 1, 0)

    lax.fori_loop(0, tiles + AHEAD, forward, 0)

    def att_copy(act, u):
        act(v == u, att_out.at[u], att_in.at[v], att_sem.at[u], att_got.at[v], (z, x, u))

    def dq_copy(act, u):
        act(v == u, dq_out.at[u], dq_in.at[v], dq_sem.at[u], dq_got.at[v], (z, x, u))

    for u in range(srv):
        at = pl.ds(u * wide, wide)
        out = (out_t[:, at] / norm[:, at]).astype(jnp.bfloat16).astype(jnp.float32)
        out_t[:, at] = out
        delta[:, at] = jnp.sum(grad_t[:, at] * out, axis=0, keepdims=True)
        top[:, at] = top[:, at] * exponent + jnp.log2(norm[:, at])

    def part_copies(act, tile):
        shard = (low_tile + tile) // blocks

        @pl.when(shard > z)
        def _():
            act(copy(part.at[tile], up_in.at[tile], part_sem.at[tile], up_got.at[tile], (z + 1, x, v)))

        @pl.when(shard < z)
        def _():
            act(copy(part.at[tile], down_in.at[tile], part_sem.at[tile], down_got.at[tile], (z - 1, x, v)))

    def grad_copies(act, least, most):
        column = pl.ds(pl.multiple_of(lane * HEAD_SIZE, HEAD_SIZE), HEAD_SIZE)

        def one(j, carry):
            @pl.when((j * piece >= least) & (j * piece < most))
            def _():
                act(
                    lane == j,
                    owned.at[:, pl.ds(pl.multiple_of(j * piece, 16), piece), :],
                    g_ref.at[:, :, column],
                    g_sem.at[j],
                    g_got.at[lane],
                    (z, j // srv, j % srv),
                )
            return carry

        lax.fori_loop(0, lanes, one, 0)

    above_first = (low_tile // blocks == z + 1) & (low_tile % blocks > 0)

    def place(i):
        tile = jnp.where(i == 0, tiles - 1, jnp.where(i <= own_first, i - 1, tiles - 1 + own_first - i))
        return jnp.where(above_first & (i >= tiles - 2), 1 - tile, tile)

    extra = (z > 0) & ((low_tile - 1) // blocks == z)
    rest = jnp.minimum(jnp.maximum(low_tile - z * blocks, 0), blocks) * TILE
    idle = jnp.where(extra, jnp.maximum(rest - TILE - piece + 1, 0), rest)

    def waits_for(tile):
        shard = (low_tile + tile) // blocks
        above = (shard >= z) & (z > 0) & (tile < tiles - 1)
        below = (shard <= z) & (z < dp - 1) & (tile > 0)
        return above, below

    def finish(tile):
        index = low_tile + tile
        shard = index // blocks

        @pl.when(shard == z)
        def _():
            row = (index - z * blocks) * TILE
            owned[:, pl.ds(pl.multiple_of(row, TILE), TILE), :] = acc[tile].astype(jnp.bfloat16)
            grad_copies(send, jnp.where(extra & (row == rest), rest - piece + 1, row), row + TILE)

        @pl.when(shard != z)
        def _():
            part[tile] = acc[tile].astype(jnp.bfloat16)
        part_copies(lambda c: c.start(), tile)

    def compute(tile):
        key_t = turned(kv_buf[tile, 0])
        values = kv_buf[tile, 1]
        key_grad = jnp.zeros((TILE, HEAD_SIZE), jnp.float32)
        value_grad = jnp.zeros((TILE, HEAD_SIZE), jnp.float32)
        for u in range(srv):
            at = pl.ds(u * wide, wide)
            probs = jnp.exp2(scores[tile, :, at] * exponent - top[:, at])
            weight_grad = contract(values, qd_buf[1, u], 1, 1)
            score_grad = (probs * (weight_grad - delta[:, at])).astype(jnp.bfloat16)
            key_grad = key_grad + contract(score_grad, qd_buf[0, u], 1, 0)
            value_grad = value_grad + contract(probs.astype(jnp.bfloat16), qd_buf[1, u], 1, 0)
            dq_t[:, at] += contract(key_t, score_grad, 1, 0)
        acc[tile, 0] = key_grad * scale
        acc[tile, 1] = value_grad

    def backward(i, carry):
        @pl.when(i < tiles)
        def _():
            tile = place(i)
            compute(tile)
            above, below = waits_for(tile)

            @pl.when(jnp.logical_not(above | below))
            def _():
                finish(tile)

        @pl.when((i >= 1) & (i <= srv))
        def _():
            u = i - 1
            att_out[u] = out_t[:, pl.ds(pl.multiple_of(u * wide, wide), wide)].T.astype(jnp.bfloat16)
            att_copy(send, u)

        @pl.when(i == tiles - 1)
        def _():
            for u in range(srv):
                dq_out[u] = (dq_t[:, pl.ds(u * wide, wide)] * scale).T.astype(jnp.bfloat16)
                dq_copy(send, u)

        @pl.when(i >= LAG)
        def _():
            tile = place(i - LAG)
            above, below = waits_for(tile)

            @pl.when(extra & (i - LAG == tiles - 1))
            def _():
                arrived(up_in.at[0], up_got.at[0])
                owned[:, pl.ds(pl.multiple_of(rest - TILE, TILE), TILE), :] = up_in[0]
                grad_copies(send, idle, rest - piece + 1)

            @pl.when(above)
            def _():
                arrived(up_in.at[tile + 1], up_got.at[tile + 1])
                acc[tile] += up_in[tile + 1].astype(jnp.float32)

            @pl.when(below)
            def _():
                arrived(down_in.at[tile - 1], down_got.at[tile - 1])
                acc[tile] += down_in[tile - 1].astype(jnp.float32)

            @pl.when(above | below)
            def _():
                finish(tile)
        return carry

    grad_copies(send, 0, idle)
    lax.fori_loop(0, tiles + LAG, backward, 0)


    for u in range(srv):
        arrived(att_in.at[u], att_got.at[u])
        by_row(att_in, att_ref, u)
    for u in range(srv):
        arrived(dq_in.at[u], dq_got.at[u])
        by_row(dq_in, dq_ref, u)
    doc_copies(sent)
    key_copies(sent)
    query_copies(sent)

    def settle(tile, carry):
        relays(lambda c: c.wait_send(), tile)
        part_copies(lambda c: c.wait_send(), tile)
        return carry

    lax.fori_loop(0, tiles, settle, 0)
    for u in range(srv):
        att_copy(sent, u)
        dq_copy(sent, u)
    grad_copies(sent, 0, blocks * TILE)
    for j in range(lanes):
        arrived(g_ref.at[:, :, pl.ds(j * HEAD_SIZE, HEAD_SIZE)], g_got.at[j])


def window_sizes(mesh_sizes, queries, keys):
    dp, heads, srv = mesh_sizes
    home, pair, width = queries.shape
    rows = keys.shape[0]
    key_total = rows * dp * heads
    longest = key_total // 2
    first = key_total - dp * home - longest
    return (dp, heads, srv, home, pair, rows, first, longest + home)


def window_fits(sizes, width):
    dp, heads, srv, home, pair, rows, first, window = sizes
    shard = rows * heads
    if width != srv * HEAD_SIZE or home != TILE or shard % TILE or first < 0 or first % TILE or window % TILE:
        return False
    if rows % HALF or rows % srv or (rows // srv) % 16 or rows % 16:
        return False
    blocks, tiles, start = shard // TILE, window // TILE, first // TILE
    for s in range(dp):
        held = set(range(start + s, start + s + tiles))
        for other in (s - 1, s + 1):
            if 0 <= other < dp:
                for tile in range(start + other, start + other + tiles):
                    beyond = tile // blocks > s if other < s else tile // blocks < s
                    owned = tile // blocks == s
                    if (beyond or owned) and tile not in held and not (owned and other < s and tile == start + other):
                        return False
                    through = tile // blocks > s if other < s else tile // blocks < s
                    if through and tile not in held:
                        return False
    return True


def local_window(sizes, queries, keys, values, output_gradient, doc_ids):
    dp, heads, srv, home, pair, rows, first, window = sizes
    width = queries.shape[2]
    wide = pair * home
    tiles = window // TILE
    piece = rows // srv
    chunks = -(-rows // TILE)

    docs = doc_ids.reshape(-1, TILE)
    vmem = pl.BlockSpec(memory_space=pltpu.VMEM)
    outside = pl.BlockSpec(memory_space=pltpu.HBM)
    sem = pltpu.SemaphoreType.DMA
    lanes = heads * srv
    b16, f32 = jnp.bfloat16, jnp.float32
    att, dq, kv = pl.pallas_call(
        functools.partial(attend, sizes),
        out_shape=(
            jax.ShapeDtypeStruct((home, pair, width), b16),
            jax.ShapeDtypeStruct((home, pair, width), b16),
            jax.ShapeDtypeStruct((2, piece, lanes * HEAD_SIZE), b16),
        ),
        in_specs=[outside] * 5,
        out_specs=(vmem, vmem, vmem),
        scratch_shapes=[
            pltpu.VMEM((2, home, pair, width), b16),
            pltpu.VMEM((srv, 2, wide, HEAD_SIZE), b16),
            pltpu.VMEM((2, srv, wide, HEAD_SIZE), b16),
            pltpu.VMEM((tiles, 2, TILE, HEAD_SIZE), b16),
            pltpu.VMEM((dp, docs.shape[0], TILE), jnp.int32),
            pltpu.VMEM((tiles, TILE, srv * wide), f32),
            pltpu.VMEM((1, srv * wide), f32),
            pltpu.VMEM((1, srv * wide), f32),
            pltpu.VMEM((1, srv * wide), f32),
            pltpu.VMEM((HEAD_SIZE, srv * wide), f32),
            pltpu.VMEM((HEAD_SIZE, srv * wide), f32),
            pltpu.VMEM((HEAD_SIZE, srv * wide), f32),
            pltpu.VMEM((tiles, 2, TILE, HEAD_SIZE), f32),
            pltpu.VMEM((tiles, 2, TILE, HEAD_SIZE), b16),
            pltpu.VMEM((tiles, 2, TILE, HEAD_SIZE), b16),
            pltpu.VMEM((tiles, 2, TILE, HEAD_SIZE), b16),
            pltpu.VMEM((2, rows * heads, HEAD_SIZE), b16),
            pltpu.VMEM((srv, wide, HEAD_SIZE), b16),
            pltpu.VMEM((srv, wide, HEAD_SIZE), b16),
            pltpu.VMEM((srv, wide, HEAD_SIZE), b16),
            pltpu.VMEM((srv, wide, HEAD_SIZE), b16),
            sem((2,)), sem((srv,)), sem((srv,)),
            sem((3 * heads, chunks, 2)), sem((tiles,)), sem((tiles,)),
            sem((dp,)), sem((dp,)),
            sem((srv,)), sem((srv,)),
            sem((srv,)), sem((srv,)),
            sem((tiles,)), sem((tiles,)), sem((tiles,)),
            sem((lanes,)), sem((lanes,)),
        ],
        compiler_params=pltpu.CompilerParams(
            collective_id=0, has_side_effects=True, vmem_limit_bytes=63 * 1024 * 1024
        ),
    )(queries, output_gradient, keys, values, docs)

    return att, dq, kv[0], kv[1]


def local_spread(queries, keys, values, output_gradient, doc_ids):
    home_rows, pair_heads, group_width = queries.shape
    groups = group_width // HEAD_SIZE
    scale_factor = HEAD_SIZE ** (-0.5)
    key_rows, value_rows = (
        lax.all_to_all(keys, "head", split_axis=1, concat_axis=0, tiled=True),
        lax.all_to_all(values, "head", split_axis=1, concat_axis=0, tiled=True),
    )
    key_count = key_rows.shape[0]
    servers = lax.axis_size("dp")
    server = lax.axis_index("dp")
    key_at = server * key_count + jnp.arange(key_count, dtype=jnp.int32)
    all_docs = lax.all_gather(doc_ids, "dp", axis=0, tiled=True)
    query_total = home_rows * servers
    context = all_docs.shape[0] - query_total
    query_docs = all_docs[context:]
    query_places = context + jnp.arange(query_total, dtype=jnp.int32)
    all_q, all_dout = (
        lax.all_gather(queries, "dp", axis=0, tiled=True),
        lax.all_gather(output_gradient, "dp", axis=0, tiled=True),
    )
    block_rows = math.gcd(512, query_total)
    block_count = query_total // block_rows
    key_heads = key_rows.reshape(key_count, groups, HEAD_SIZE)
    value_heads = value_rows.reshape(key_count, groups, HEAD_SIZE)
    query_blocks = all_q.reshape(block_count, block_rows, pair_heads, groups, HEAD_SIZE)
    grad_blocks = all_dout.reshape(block_count, block_rows, pair_heads, groups, HEAD_SIZE)
    place_blocks = query_places.reshape(block_count, block_rows)
    doc_blocks = query_docs.reshape(block_count, block_rows)

    def admissible(places, query_doc):
        return (key_at[None, :] <= places[:, None]) & (doc_ids[None, :] == query_doc[:, None])

    def scores_of(query_block):
        return (
            jnp.einsum("pjgd,kgd->gjpk", query_block, key_heads, preferred_element_type=jnp.float32)
            * scale_factor
        )

    def block_max(inputs):
        query_block, places, query_doc = inputs
        allowed = admissible(places, query_doc)

        def compute():
            raw_scores = scores_of(query_block)
            masked = jnp.where(allowed[None, None], raw_scores, NEGATIVE)
            return (jnp.max(masked, axis=-1).transpose(2, 1, 0), raw_scores)

        return compute()

    def block_top(inputs):
        return block_max(inputs)[0]

    local_max = lax.map(block_top, (query_blocks, place_blocks, doc_blocks))
    row_max = lax.pmax(local_max.reshape(query_total, pair_heads, groups), "dp")
    max_blocks = row_max.reshape(block_count, block_rows, pair_heads, groups)

    def block_sum(inputs):
        stored, places, query_doc, row_top = inputs
        allowed = admissible(places, query_doc)

        def compute():
            block_scores = scores_of(stored)
            shifted = block_scores - row_top.transpose(2, 1, 0)[..., None]
            weights = jnp.where(allowed[None, None], jnp.exp(shifted), 0.0)
            weighted = jnp.einsum(
                "gjpk,kgd->pjgd",
                weights.astype(jnp.bfloat16),
                value_heads,
                preferred_element_type=jnp.float32,
            )
            return (
                weighted.reshape(block_rows, pair_heads, group_width),
                jnp.sum(weights, axis=-1).transpose(2, 1, 0),
            )

        return compute()

    part_out, part_norm = lax.map(block_sum, (query_blocks, place_blocks, doc_blocks, max_blocks))
    part_out = part_out.reshape(query_total, pair_heads, group_width)
    part_norm = part_norm.reshape(query_total, pair_heads, groups)
    home_out, home_norm = (
        lax.psum_scatter(part_out, "dp", scatter_dimension=0, tiled=True),
        lax.psum_scatter(part_norm, "dp", scatter_dimension=0, tiled=True),
    )
    home_max = lax.dynamic_slice_in_dim(row_max, server * home_rows, home_rows, 0)
    attn_home = (
        home_out.reshape(home_rows, pair_heads, groups, HEAD_SIZE) / home_norm[..., None]
    ).astype(jnp.bfloat16)
    log_home = home_max + jnp.log(home_norm)
    grad_home = output_gradient.reshape(home_rows, pair_heads, groups, HEAD_SIZE).astype(
        jnp.float32
    )
    delta_home = jnp.sum(grad_home * attn_home.astype(jnp.float32), axis=-1)
    log_all, delta_all = (
        lax.all_gather(log_home, "dp", axis=0, tiled=True),
        lax.all_gather(delta_home, "dp", axis=0, tiled=True),
    )
    attention = attn_home.reshape(home_rows, pair_heads, group_width)
    log_blocks = log_all.reshape(block_count, block_rows, pair_heads, groups)
    delta_blocks = delta_all.reshape(block_count, block_rows, pair_heads, groups)

    def block_grad(totals, inputs):
        query_block, grad_block, places, query_doc, log_norm, row_delta = inputs
        allowed = admissible(places, query_doc)

        def compute():
            shifted = scores_of(query_block) - log_norm.transpose(2, 1, 0)[..., None]
            probs = jnp.where(allowed[None, None], jnp.exp(shifted), 0.0)
            value_grad = jnp.einsum(
                "gjpk,pjgd->kgd",
                probs.astype(jnp.bfloat16),
                grad_block,
                preferred_element_type=jnp.float32,
            )
            weight_grad = jnp.einsum(
                "pjgd,kgd->gjpk", grad_block, value_heads, preferred_element_type=jnp.float32
            )
            score_grad = (probs * (weight_grad - row_delta.transpose(2, 1, 0)[..., None])).astype(
                jnp.bfloat16
            )
            query_grad = (
                jnp.einsum(
                    "gjpk,kgd->pjgd", score_grad, key_heads, preferred_element_type=jnp.float32
                )
                * scale_factor
            )
            key_grad = (
                jnp.einsum(
                    "gjpk,pjgd->kgd", score_grad, query_block, preferred_element_type=jnp.float32
                )
                * scale_factor
            )
            return (query_grad.reshape(block_rows, pair_heads, group_width), key_grad, value_grad)

        query_grad, key_grad, value_grad = compute()
        return ((totals[0] + key_grad, totals[1] + value_grad), query_grad)

    zero_start = jnp.zeros((key_count, groups, HEAD_SIZE), jnp.float32)
    grad_inputs = (query_blocks, grad_blocks, place_blocks, doc_blocks, log_blocks, delta_blocks)
    (key_total, value_total), query_parts = lax.scan(
        block_grad, (zero_start, zero_start), grad_inputs
    )
    q_summed = lax.psum_scatter(
        query_parts.reshape(query_total, pair_heads, group_width).astype(jnp.bfloat16),
        "dp",
        scatter_dimension=0,
        tiled=True,
    )
    spread_key, spread_value = (
        lax.all_to_all(
            key_total.reshape(key_count, group_width).astype(jnp.bfloat16),
            "head",
            split_axis=0,
            concat_axis=1,
            tiled=True,
        ).astype(jnp.float32),
        lax.all_to_all(
            value_total.reshape(key_count, group_width).astype(jnp.bfloat16),
            "head",
            split_axis=0,
            concat_axis=1,
            tiled=True,
        ).astype(jnp.float32),
    )
    k_summed, v_summed = (
        lax.psum_scatter(
            spread_key.astype(jnp.bfloat16), "srv", scatter_dimension=0, tiled=True
        ).astype(jnp.float32),
        lax.psum_scatter(
            spread_value.astype(jnp.bfloat16), "srv", scatter_dimension=0, tiled=True
        ).astype(jnp.float32),
    )
    return (attention, q_summed, k_summed.astype(jnp.bfloat16), v_summed.astype(jnp.bfloat16))


def solution(mesh):
    placed = (
        P("dp", "srv", "head"),
        P(("dp", "head"), None),
        P(("dp", "head"), None),
        P("dp", "srv", "head"),
        P("dp"),
    )
    mesh_sizes = tuple(mesh.shape[name] for name in AXES)

    def local(queries, keys, values, output_gradient, doc_ids):
        args = (queries, keys, values, output_gradient, doc_ids)
        sizes = window_sizes(mesh_sizes, queries, keys)
        if window_fits(sizes, queries.shape[2]):
            return local_window(sizes, *args)
        return local_spread(*args)

    return jax.shard_map(
        local,
        mesh=mesh,
        in_specs=placed,
        out_specs=(
            P("dp", "srv", "head"),
            P("dp", "srv", "head"),
            P(("dp", "head", "srv"), None),
            P(("dp", "head", "srv"), None),
        ),
        check_vma=False,
    )
```

```python
import functools
import math

import jax
import jax.numpy as jnp
from jax import lax
from jax.experimental import pallas as pl
from jax.experimental.pallas import tpu as pltpu
from jax.sharding import PartitionSpec as P

HEAD_SIZE = 128


NEGATIVE = -1e30
MESH = pl.DeviceIdType.MESH
AXES = ("dp", "head", "srv")


TILE = 128
HALF = 64
LAG = 3
AHEAD = 3


def attend(sizes, q_ref, o_ref, k_ref, v_ref, doc_ref, att_ref, dq_ref, g_ref,
           raw, stage, qd_buf, kv_buf, docs, scores, top, norm, delta, out_t, grad_t, dq_t, acc, part, up_in, down_in, owned, att_out, dq_out, att_in, dq_in,
           raw_got, q_sem, q_got, kv_sem, kv_got, relay_sem, doc_sem, doc_got, att_sem, att_got, dq_sem, dq_got,
           part_sem, up_got, down_got, g_sem, g_got):
    dp, heads, srv, home, pair, rows, first, window = sizes
    piece = rows // srv
    wide = pair * home
    every = srv * wide
    tiles = window // TILE
    blocks = rows * heads // TILE
    lanes = heads * srv
    scale = HEAD_SIZE ** (-0.5)
    exponent = scale * math.log2(math.e)
    z, x, v = (lax.axis_index(name) for name in AXES)
    base = (z * heads + x) * rows
    low = first + home * z
    low_tile = low // TILE
    own_first = jnp.maximum(z * blocks - low_tile, 0)
    lane = x * srv + v

    def copy(src, dst, send_sem, recv_sem, target):
        return pltpu.make_async_remote_copy(
            src_ref=src, dst_ref=dst, send_sem=send_sem, recv_sem=recv_sem,
            device_id=target, device_id_type=MESH,
        )

    def send(here, src, dst, send_sem, recv_sem, target):
        @pl.when(here)
        def _():
            pltpu.make_async_copy(src, dst, recv_sem).start()

        @pl.when(jnp.logical_not(here))
        def _():
            copy(src, dst, send_sem, recv_sem, target).start()

    def sent(here, src, dst, send_sem, recv_sem, target):
        @pl.when(jnp.logical_not(here))
        def _():
            copy(src, dst, send_sem, recv_sem, target).wait_send()

    def arrived(ref, sem):
        pltpu.make_async_copy(ref, ref, sem).wait()

    for which, ref in ((0, q_ref), (1, o_ref)):
        pltpu.make_async_copy(ref, raw.at[which], raw_got.at[which]).start()

    def stage_queries():
        for which in range(2):
            arrived(raw.at[which], raw_got.at[which])
            for u in range(srv):
                block = raw[which, :, :, pl.ds(u * HEAD_SIZE, HEAD_SIZE)].astype(jnp.float32)
                for j in range(pair):
                    stage[u, which, pl.ds(j * home, home), :] = block[:, j, :].astype(jnp.bfloat16)

    def by_row(source, target, u):
        heads_of = [source[u, pl.ds(j * home, home), :].astype(jnp.float32) for j in range(pair)]
        target[:, :, pl.ds(u * HEAD_SIZE, HEAD_SIZE)] = jnp.stack(heads_of, axis=1).astype(jnp.bfloat16)

    barrier = pltpu.get_barrier_semaphore()

    def greet(s, h, u):
        pl.semaphore_signal(barrier, inc=1, device_id=(s, h, u), device_id_type=MESH)

    for step in range(1, dp):
        greet((z + step) % dp, x, v)
    for step in range(1, heads):
        @pl.when(z > 0)
        def _():
            greet(z - 1, (x + step) % heads, v)

        @pl.when(z < dp - 1)
        def _():
            greet(z + 1, (x + step) % heads, v)
    for step in range(1, lanes):
        other = (lane + step) % lanes
        greet(z, other // srv, other % srv)
    sides = jnp.where(z > 0, 1, 0) + jnp.where(z < dp - 1, 1, 0)
    pl.semaphore_wait(barrier, lanes - 1 + sides * heads + dp - 1 - sides)

    def key_copies(act):
        def one(index, carry):
            side, h = index // heads, (x + index) % heads
            s = z + side - 1
            column = pl.ds(pl.multiple_of((h * srv + v) * HEAD_SIZE, HEAD_SIZE), HEAD_SIZE)
            start = first + home * s

            def each(at, count, slot):
                row = base + at - start

                @pl.when((s >= 0) & (s < dp) & (row >= 0) & (row < window))
                def _():
                    for which, ref in ((0, k_ref), (1, v_ref)):
                        act(
                            (s == z) & (h == x),
                            ref.at[pl.ds(pl.multiple_of(at, HALF), count), column],
                            kv_buf.at[row // TILE, which, pl.ds(pl.multiple_of(row % TILE, count), count), :],
                            kv_sem.at[index, slot, which],
                            kv_got.at[row // TILE],
                            (s, h, v),
                        )

            for c in range(rows // TILE):
                each(c * TILE + base % TILE, TILE, c)
            if rows % TILE:
                each(jnp.where(base % TILE == 0, rows - HALF, 0), HALF, rows // TILE)
            return carry

        lax.fori_loop(0, 3 * heads, one, 0)

    def doc_copies(act):
        for s in range(dp):
            act(z == s, doc_ref, docs.at[z], doc_sem.at[s], doc_got.at[z], (s, x, v))

    def query_copies(act):
        for u in range(srv):
            act(v == u, stage.at[u], qd_buf.at[:, v], q_sem.at[u], q_got.at[v], (z, x, u))

    key_copies(send)
    doc_copies(send)
    stage_queries()
    query_copies(send)

    top[...] = jnp.full_like(top, NEGATIVE / 10)
    norm[...] = jnp.zeros_like(norm)
    out_t[...] = jnp.zeros_like(out_t)
    dq_t[...] = jnp.zeros_like(dq_t)
    owned[...] = jnp.zeros_like(owned)

    def contract(a, b, left, right):
        return lax.dot_general(a, b, (((left,), (right,)), ((), ())), preferred_element_type=jnp.float32)

    def turned(a):
        return a.astype(jnp.float32).T.astype(jnp.bfloat16)

    for s in range(dp):
        arrived(docs.at[s], doc_got.at[s])
    home_tile = low_tile + tiles - 1
    query_doc = docs[home_tile // blocks, pl.ds(home_tile % blocks, 1), :]
    query_doc = jnp.broadcast_to(query_doc.astype(jnp.float32), (TILE, home))
    query_at = lax.broadcasted_iota(jnp.int32, (TILE, home), 1) + home_tile * TILE
    for u in range(srv):
        arrived(qd_buf.at[:, u], q_got.at[u])
        grad_t[:, pl.ds(u * wide, wide)] = qd_buf[1, u].astype(jnp.float32).T

    def relays(act, tile):
        shard = (low_tile + tile) // blocks

        @pl.when((shard > z) & (z > 0) & (tile < tiles - 1))
        def _():
            act(copy(kv_buf.at[tile], kv_buf.at[tile + 1], relay_sem.at[tile], kv_got.at[tile + 1], (z - 1, x, v)))

        @pl.when((shard < z) & (z < dp - 1) & (tile > 0))
        def _():
            act(copy(kv_buf.at[tile], kv_buf.at[tile - 1], relay_sem.at[tile], kv_got.at[tile - 1], (z + 1, x, v)))

    ahead = jnp.where((z > 0) & (z < dp - 1), AHEAD, 0)

    def forward(i, carry):
        def turn(i):
            return jnp.where(i < tiles - own_first, own_first + i, tiles - 1 - i)

        @pl.when(i < tiles)
        def _():
            tile = turn(i)
            arrived(kv_buf.at[tile], kv_got.at[tile])
            relays(lambda c: c.start(), tile)

        @pl.when((i >= ahead) & (i < tiles + ahead))
        def _():
            meet(turn(i - ahead))
        return carry

    def meet(tile):
        index = low_tile + tile
        key_doc = docs[index // blocks, pl.ds(index % blocks, 1), :]
        key_doc = jnp.broadcast_to(key_doc.astype(jnp.float32), (TILE, TILE)).T
        key_at = lax.broadcasted_iota(jnp.int32, (TILE, home), 0) + index * TILE
        bias = jnp.where((key_doc == query_doc) & (key_at <= query_at), 0.0, NEGATIVE)
        value_t = turned(kv_buf[tile, 1])
        keys = kv_buf[tile, 0]
        for u in range(srv):
            at = pl.ds(u * wide, wide)
            raw = contract(keys, qd_buf[0, u], 1, 1) + jnp.concatenate([bias] * pair, axis=1)
            scores[tile, :, at] = raw
            old = top[:, at]
            new = jnp.maximum(old, jnp.max(raw, axis=0, keepdims=True))
            weights = jnp.exp2((raw - new) * exponent)
            shrink = jnp.exp2((old - new) * exponent)
            top[:, at] = new
            norm[:, at] = norm[:, at] * shrink + jnp.sum(weights, axis=0, keepdims=True)
            out_t[:, at] = out_t[:, at] * shrink + contract(value_t, weights.astype(jnp.bfloat16), 1, 0)

    lax.fori_loop(0, tiles + AHEAD, forward, 0)

    def att_copy(act, u):
        act(v == u, att_out.at[u], att_in.at[v], att_sem.at[u], att_got.at[v], (z, x, u))

    def dq_copy(act, u):
        act(v == u, dq_out.at[u], dq_in.at[v], dq_sem.at[u], dq_got.at[v], (z, x, u))

    for u in range(srv):
        at = pl.ds(u * wide, wide)
        out = (out_t[:, at] / norm[:, at]).astype(jnp.bfloat16).astype(jnp.float32)
        out_t[:, at] = out
        delta[:, at] = jnp.sum(grad_t[:, at] * out, axis=0, keepdims=True)
        top[:, at] = top[:, at] * exponent + jnp.log2(norm[:, at])

    def part_copies(act, tile):
        shard = (low_tile + tile) // blocks

        @pl.when(shard > z)
        def _():
            act(copy(part.at[tile], up_in.at[tile], part_sem.at[tile], up_got.at[tile], (z + 1, x, v)))

        @pl.when(shard < z)
        def _():
            act(copy(part.at[tile], down_in.at[tile], part_sem.at[tile], down_got.at[tile], (z - 1, x, v)))

    def grad_copies(act, least, most):
        column = pl.ds(pl.multiple_of(lane * HEAD_SIZE, HEAD_SIZE), HEAD_SIZE)

        def one(j, carry):
            @pl.when((j * piece >= least) & (j * piece < most))
            def _():
                act(
                    lane == j,
                    owned.at[:, pl.ds(pl.multiple_of(j * piece, 16), piece), :],
                    g_ref.at[:, :, column],
                    g_sem.at[j],
                    g_got.at[lane],
                    (z, j // srv, j % srv),
                )
            return carry

        lax.fori_loop(0, lanes, one, 0)

    above_first = (low_tile // blocks == z + 1) & (low_tile % blocks > 0)

    def place(i):
        tile = jnp.where(i == 0, tiles - 1, jnp.where(i <= own_first, i - 1, tiles - 1 + own_first - i))
        return jnp.where(above_first & (i >= tiles - 2), 1 - tile, tile)

    extra = (z > 0) & ((low_tile - 1) // blocks == z)
    rest = jnp.minimum(jnp.maximum(low_tile - z * blocks, 0), blocks) * TILE
    idle = jnp.where(extra, jnp.maximum(rest - TILE - piece + 1, 0), rest)

    def waits_for(tile):
        shard = (low_tile + tile) // blocks
        above = (shard >= z) & (z > 0) & (tile < tiles - 1)
        below = (shard <= z) & (z < dp - 1) & (tile > 0)
        return above, below

    def finish(tile):
        index = low_tile + tile
        shard = index // blocks

        @pl.when(shard == z)
        def _():
            row = (index - z * blocks) * TILE
            owned[:, pl.ds(pl.multiple_of(row, TILE), TILE), :] = acc[tile].astype(jnp.bfloat16)
            grad_copies(send, jnp.where(extra & (row == rest), rest - piece + 1, row), row + TILE)

        @pl.when(shard != z)
        def _():
            part[tile] = acc[tile].astype(jnp.bfloat16)
        part_copies(lambda c: c.start(), tile)

    def compute(tile):
        key_t = turned(kv_buf[tile, 0])
        values = kv_buf[tile, 1]
        all_probs, all_grads = [], []
        for u in range(srv):
            at = pl.ds(u * wide, wide)
            probs = jnp.exp2(scores[tile, :, at] * exponent - top[:, at])
            weight_grad = contract(values, qd_buf[1, u], 1, 1)
            all_grads.append((probs * (weight_grad - delta[:, at])).astype(jnp.bfloat16))
            all_probs.append(probs.astype(jnp.bfloat16))
            dq_t[:, at] += contract(key_t, all_grads[-1], 1, 0)
        flat = (srv * wide, HEAD_SIZE)
        acc[tile, 0] = contract(jnp.concatenate(all_grads, axis=1), qd_buf[0].reshape(flat), 1, 0) * scale
        acc[tile, 1] = contract(jnp.concatenate(all_probs, axis=1), qd_buf[1].reshape(flat), 1, 0)

    def backward(i, carry):
        @pl.when(i < tiles)
        def _():
            tile = place(i)
            compute(tile)
            above, below = waits_for(tile)

            @pl.when(jnp.logical_not(above | below))
            def _():
                finish(tile)

        @pl.when((i >= 1) & (i <= srv))
        def _():
            u = i - 1
            att_out[u] = out_t[:, pl.ds(pl.multiple_of(u * wide, wide), wide)].T.astype(jnp.bfloat16)
            att_copy(send, u)

        @pl.when(i == tiles - 1)
        def _():
            for u in range(srv):
                dq_out[u] = (dq_t[:, pl.ds(u * wide, wide)] * scale).T.astype(jnp.bfloat16)
                dq_copy(send, u)
            for u in range(srv):
                arrived(att_in.at[u], att_got.at[u])
                by_row(att_in, att_ref, u)

        @pl.when(i == tiles + LAG - 2)
        def _():
            for u in range(srv):
                arrived(dq_in.at[u], dq_got.at[u])
                by_row(dq_in, dq_ref, u)

        @pl.when(i >= LAG)
        def _():
            tile = place(i - LAG)
            above, below = waits_for(tile)

            @pl.when(extra & (i - LAG == tiles - 1))
            def _():
                arrived(up_in.at[0], up_got.at[0])
                owned[:, pl.ds(pl.multiple_of(rest - TILE, TILE), TILE), :] = up_in[0]
                grad_copies(send, idle, rest - piece + 1)

            @pl.when(above)
            def _():
                arrived(up_in.at[tile + 1], up_got.at[tile + 1])
                acc[tile] += up_in[tile + 1].astype(jnp.float32)

            @pl.when(below)
            def _():
                arrived(down_in.at[tile - 1], down_got.at[tile - 1])
                acc[tile] += down_in[tile - 1].astype(jnp.float32)

            @pl.when(above | below)
            def _():
                finish(tile)
        return carry

    grad_copies(send, 0, idle)
    lax.fori_loop(0, tiles + LAG, backward, 0)


    doc_copies(sent)
    key_copies(sent)
    query_copies(sent)

    def settle(tile, carry):
        relays(lambda c: c.wait_send(), tile)
        part_copies(lambda c: c.wait_send(), tile)
        return carry

    lax.fori_loop(0, tiles, settle, 0)
    for u in range(srv):
        att_copy(sent, u)
        dq_copy(sent, u)
    grad_copies(sent, 0, blocks * TILE)
    for j in range(lanes):
        arrived(g_ref.at[:, :, pl.ds(j * HEAD_SIZE, HEAD_SIZE)], g_got.at[j])


def window_sizes(mesh_sizes, queries, keys):
    dp, heads, srv = mesh_sizes
    home, pair, width = queries.shape
    rows = keys.shape[0]
    key_total = rows * dp * heads
    longest = key_total // 2
    first = key_total - dp * home - longest
    return (dp, heads, srv, home, pair, rows, first, longest + home)


def window_fits(sizes, width):
    dp, heads, srv, home, pair, rows, first, window = sizes
    shard = rows * heads
    if width != srv * HEAD_SIZE or home != TILE or shard % TILE or first < 0 or first % TILE or window % TILE:
        return False
    if rows % HALF or rows % srv or (rows // srv) % 16 or rows % 16:
        return False
    blocks, tiles, start = shard // TILE, window // TILE, first // TILE
    for s in range(dp):
        held = set(range(start + s, start + s + tiles))
        for other in (s - 1, s + 1):
            if 0 <= other < dp:
                for tile in range(start + other, start + other + tiles):
                    beyond = tile // blocks > s if other < s else tile // blocks < s
                    owned = tile // blocks == s
                    if (beyond or owned) and tile not in held and not (owned and other < s and tile == start + other):
                        return False
                    through = tile // blocks > s if other < s else tile // blocks < s
                    if through and tile not in held:
                        return False
    return True


def local_window(sizes, queries, keys, values, output_gradient, doc_ids):
    dp, heads, srv, home, pair, rows, first, window = sizes
    width = queries.shape[2]
    wide = pair * home
    tiles = window // TILE
    piece = rows // srv
    chunks = -(-rows // TILE)

    docs = doc_ids.reshape(-1, TILE)
    vmem = pl.BlockSpec(memory_space=pltpu.VMEM)
    outside = pl.BlockSpec(memory_space=pltpu.HBM)
    sem = pltpu.SemaphoreType.DMA
    lanes = heads * srv
    b16, f32 = jnp.bfloat16, jnp.float32
    att, dq, kv = pl.pallas_call(
        functools.partial(attend, sizes),
        out_shape=(
            jax.ShapeDtypeStruct((home, pair, width), b16),
            jax.ShapeDtypeStruct((home, pair, width), b16),
            jax.ShapeDtypeStruct((2, piece, lanes * HEAD_SIZE), b16),
        ),
        in_specs=[outside] * 5,
        out_specs=(vmem, vmem, vmem),
        scratch_shapes=[
            pltpu.VMEM((2, home, pair, width), b16),
            pltpu.VMEM((srv, 2, wide, HEAD_SIZE), b16),
            pltpu.VMEM((2, srv, wide, HEAD_SIZE), b16),
            pltpu.VMEM((tiles, 2, TILE, HEAD_SIZE), b16),
            pltpu.VMEM((dp, docs.shape[0], TILE), jnp.int32),
            pltpu.VMEM((tiles, TILE, srv * wide), f32),
            pltpu.VMEM((1, srv * wide), f32),
            pltpu.VMEM((1, srv * wide), f32),
            pltpu.VMEM((1, srv * wide), f32),
            pltpu.VMEM((HEAD_SIZE, srv * wide), f32),
            pltpu.VMEM((HEAD_SIZE, srv * wide), f32),
            pltpu.VMEM((HEAD_SIZE, srv * wide), f32),
            pltpu.VMEM((tiles, 2, TILE, HEAD_SIZE), f32),
            pltpu.VMEM((tiles, 2, TILE, HEAD_SIZE), b16),
            pltpu.VMEM((tiles, 2, TILE, HEAD_SIZE), b16),
            pltpu.VMEM((tiles, 2, TILE, HEAD_SIZE), b16),
            pltpu.VMEM((2, rows * heads, HEAD_SIZE), b16),
            pltpu.VMEM((srv, wide, HEAD_SIZE), b16),
            pltpu.VMEM((srv, wide, HEAD_SIZE), b16),
            pltpu.VMEM((srv, wide, HEAD_SIZE), b16),
            pltpu.VMEM((srv, wide, HEAD_SIZE), b16),
            sem((2,)), sem((srv,)), sem((srv,)),
            sem((3 * heads, chunks, 2)), sem((tiles,)), sem((tiles,)),
            sem((dp,)), sem((dp,)),
            sem((srv,)), sem((srv,)),
            sem((srv,)), sem((srv,)),
            sem((tiles,)), sem((tiles,)), sem((tiles,)),
            sem((lanes,)), sem((lanes,)),
        ],
        compiler_params=pltpu.CompilerParams(
            collective_id=0, has_side_effects=True, vmem_limit_bytes=63 * 1024 * 1024
        ),
    )(queries, output_gradient, keys, values, docs)

    return att, dq, kv[0], kv[1]


def local_spread(queries, keys, values, output_gradient, doc_ids):
    home_rows, pair_heads, group_width = queries.shape
    groups = group_width // HEAD_SIZE
    scale_factor = HEAD_SIZE ** (-0.5)
    key_rows, value_rows = (
        lax.all_to_all(keys, "head", split_axis=1, concat_axis=0, tiled=True),
        lax.all_to_all(values, "head", split_axis=1, concat_axis=0, tiled=True),
    )
    key_count = key_rows.shape[0]
    servers = lax.axis_size("dp")
    server = lax.axis_index("dp")
    key_at = server * key_count + jnp.arange(key_count, dtype=jnp.int32)
    all_docs = lax.all_gather(doc_ids, "dp", axis=0, tiled=True)
    query_total = home_rows * servers
    context = all_docs.shape[0] - query_total
    query_docs = all_docs[context:]
    query_places = context + jnp.arange(query_total, dtype=jnp.int32)
    all_q, all_dout = (
        lax.all_gather(queries, "dp", axis=0, tiled=True),
        lax.all_gather(output_gradient, "dp", axis=0, tiled=True),
    )
    block_rows = math.gcd(512, query_total)
    block_count = query_total // block_rows
    key_heads = key_rows.reshape(key_count, groups, HEAD_SIZE)
    value_heads = value_rows.reshape(key_count, groups, HEAD_SIZE)
    query_blocks = all_q.reshape(block_count, block_rows, pair_heads, groups, HEAD_SIZE)
    grad_blocks = all_dout.reshape(block_count, block_rows, pair_heads, groups, HEAD_SIZE)
    place_blocks = query_places.reshape(block_count, block_rows)
    doc_blocks = query_docs.reshape(block_count, block_rows)

    def admissible(places, query_doc):
        return (key_at[None, :] <= places[:, None]) & (doc_ids[None, :] == query_doc[:, None])

    def scores_of(query_block):
        return (
            jnp.einsum("pjgd,kgd->gjpk", query_block, key_heads, preferred_element_type=jnp.float32)
            * scale_factor
        )

    def block_max(inputs):
        query_block, places, query_doc = inputs
        allowed = admissible(places, query_doc)

        def compute():
            raw_scores = scores_of(query_block)
            masked = jnp.where(allowed[None, None], raw_scores, NEGATIVE)
            return (jnp.max(masked, axis=-1).transpose(2, 1, 0), raw_scores)

        return compute()

    def block_top(inputs):
        return block_max(inputs)[0]

    local_max = lax.map(block_top, (query_blocks, place_blocks, doc_blocks))
    row_max = lax.pmax(local_max.reshape(query_total, pair_heads, groups), "dp")
    max_blocks = row_max.reshape(block_count, block_rows, pair_heads, groups)

    def block_sum(inputs):
        stored, places, query_doc, row_top = inputs
        allowed = admissible(places, query_doc)

        def compute():
            block_scores = scores_of(stored)
            shifted = block_scores - row_top.transpose(2, 1, 0)[..., None]
            weights = jnp.where(allowed[None, None], jnp.exp(shifted), 0.0)
            weighted = jnp.einsum(
                "gjpk,kgd->pjgd",
                weights.astype(jnp.bfloat16),
                value_heads,
                preferred_element_type=jnp.float32,
            )
            return (
                weighted.reshape(block_rows, pair_heads, group_width),
                jnp.sum(weights, axis=-1).transpose(2, 1, 0),
            )

        return compute()

    part_out, part_norm = lax.map(block_sum, (query_blocks, place_blocks, doc_blocks, max_blocks))
    part_out = part_out.reshape(query_total, pair_heads, group_width)
    part_norm = part_norm.reshape(query_total, pair_heads, groups)
    home_out, home_norm = (
        lax.psum_scatter(part_out, "dp", scatter_dimension=0, tiled=True),
        lax.psum_scatter(part_norm, "dp", scatter_dimension=0, tiled=True),
    )
    home_max = lax.dynamic_slice_in_dim(row_max, server * home_rows, home_rows, 0)
    attn_home = (
        home_out.reshape(home_rows, pair_heads, groups, HEAD_SIZE) / home_norm[..., None]
    ).astype(jnp.bfloat16)
    log_home = home_max + jnp.log(home_norm)
    grad_home = output_gradient.reshape(home_rows, pair_heads, groups, HEAD_SIZE).astype(
        jnp.float32
    )
    delta_home = jnp.sum(grad_home * attn_home.astype(jnp.float32), axis=-1)
    log_all, delta_all = (
        lax.all_gather(log_home, "dp", axis=0, tiled=True),
        lax.all_gather(delta_home, "dp", axis=0, tiled=True),
    )
    attention = attn_home.reshape(home_rows, pair_heads, group_width)
    log_blocks = log_all.reshape(block_count, block_rows, pair_heads, groups)
    delta_blocks = delta_all.reshape(block_count, block_rows, pair_heads, groups)

    def block_grad(totals, inputs):
        query_block, grad_block, places, query_doc, log_norm, row_delta = inputs
        allowed = admissible(places, query_doc)

        def compute():
            shifted = scores_of(query_block) - log_norm.transpose(2, 1, 0)[..., None]
            probs = jnp.where(allowed[None, None], jnp.exp(shifted), 0.0)
            value_grad = jnp.einsum(
                "gjpk,pjgd->kgd",
                probs.astype(jnp.bfloat16),
                grad_block,
                preferred_element_type=jnp.float32,
            )
            weight_grad = jnp.einsum(
                "pjgd,kgd->gjpk", grad_block, value_heads, preferred_element_type=jnp.float32
            )
            score_grad = (probs * (weight_grad - row_delta.transpose(2, 1, 0)[..., None])).astype(
                jnp.bfloat16
            )
            query_grad = (
                jnp.einsum(
                    "gjpk,kgd->pjgd", score_grad, key_heads, preferred_element_type=jnp.float32
                )
                * scale_factor
            )
            key_grad = (
                jnp.einsum(
                    "gjpk,pjgd->kgd", score_grad, query_block, preferred_element_type=jnp.float32
                )
                * scale_factor
            )
            return (query_grad.reshape(block_rows, pair_heads, group_width), key_grad, value_grad)

        query_grad, key_grad, value_grad = compute()
        return ((totals[0] + key_grad, totals[1] + value_grad), query_grad)

    zero_start = jnp.zeros((key_count, groups, HEAD_SIZE), jnp.float32)
    grad_inputs = (query_blocks, grad_blocks, place_blocks, doc_blocks, log_blocks, delta_blocks)
    (key_total, value_total), query_parts = lax.scan(
        block_grad, (zero_start, zero_start), grad_inputs
    )
    q_summed = lax.psum_scatter(
        query_parts.reshape(query_total, pair_heads, group_width).astype(jnp.bfloat16),
        "dp",
        scatter_dimension=0,
        tiled=True,
    )
    spread_key, spread_value = (
        lax.all_to_all(
            key_total.reshape(key_count, group_width).astype(jnp.bfloat16),
            "head",
            split_axis=0,
            concat_axis=1,
            tiled=True,
        ).astype(jnp.float32),
        lax.all_to_all(
            value_total.reshape(key_count, group_width).astype(jnp.bfloat16),
            "head",
            split_axis=0,
            concat_axis=1,
            tiled=True,
        ).astype(jnp.float32),
    )
    k_summed, v_summed = (
        lax.psum_scatter(
            spread_key.astype(jnp.bfloat16), "srv", scatter_dimension=0, tiled=True
        ).astype(jnp.float32),
        lax.psum_scatter(
            spread_value.astype(jnp.bfloat16), "srv", scatter_dimension=0, tiled=True
        ).astype(jnp.float32),
    )
    return (attention, q_summed, k_summed.astype(jnp.bfloat16), v_summed.astype(jnp.bfloat16))


def solution(mesh):
    placed = (
        P("dp", "srv", "head"),
        P(("dp", "head"), None),
        P(("dp", "head"), None),
        P("dp", "srv", "head"),
        P("dp"),
    )
    mesh_sizes = tuple(mesh.shape[name] for name in AXES)

    def local(queries, keys, values, output_gradient, doc_ids):
        args = (queries, keys, values, output_gradient, doc_ids)
        sizes = window_sizes(mesh_sizes, queries, keys)
        if window_fits(sizes, queries.shape[2]):
            return local_window(sizes, *args)
        return local_spread(*args)

    return jax.shard_map(
        local,
        mesh=mesh,
        in_specs=placed,
        out_specs=(
            P("dp", "srv", "head"),
            P("dp", "srv", "head"),
            P(("dp", "head", "srv"), None),
            P(("dp", "head", "srv"), None),
        ),
        check_vma=False,
    )
```

```python
import functools
import math

import jax
import jax.numpy as jnp
from jax import lax
from jax.experimental import pallas as pl
from jax.experimental.pallas import tpu as pltpu
from jax.sharding import PartitionSpec as P

HEAD_SIZE = 128


NEGATIVE = -1e30
MESH = pl.DeviceIdType.MESH
AXES = ("dp", "head", "srv")


TILE = 128
HALF = 64
LAG = 3
AHEAD = 3


def attend(sizes, q_ref, o_ref, k_ref, v_ref, doc_ref, att_ref, dq_ref, g_ref,
           raw, stage, qd_buf, kv_buf, docs, scores, top, norm, delta, out_t, grad_t, dq_t, acc, part, up_in, down_in, owned, att_out, dq_out, att_in, dq_in,
           raw_got, q_sem, q_got, kv_sem, kv_got, relay_sem, doc_sem, doc_got, att_sem, att_got, dq_sem, dq_got,
           part_sem, up_got, down_got, g_sem, g_got):
    dp, heads, srv, home, pair, rows, first, window = sizes
    piece = rows // srv
    wide = pair * home
    every = srv * wide
    tiles = window // TILE
    blocks = rows * heads // TILE
    lanes = heads * srv
    scale = HEAD_SIZE ** (-0.5)
    exponent = scale * math.log2(math.e)
    z, x, v = (lax.axis_index(name) for name in AXES)
    base = (z * heads + x) * rows
    low = first + home * z
    low_tile = low // TILE
    own_first = jnp.maximum(z * blocks - low_tile, 0)
    lane = x * srv + v

    def copy(src, dst, send_sem, recv_sem, target):
        return pltpu.make_async_remote_copy(
            src_ref=src, dst_ref=dst, send_sem=send_sem, recv_sem=recv_sem,
            device_id=target, device_id_type=MESH,
        )

    def send(here, src, dst, send_sem, recv_sem, target):
        @pl.when(here)
        def _():
            pltpu.make_async_copy(src, dst, recv_sem).start()

        @pl.when(jnp.logical_not(here))
        def _():
            copy(src, dst, send_sem, recv_sem, target).start()

    def sent(here, src, dst, send_sem, recv_sem, target):
        @pl.when(jnp.logical_not(here))
        def _():
            copy(src, dst, send_sem, recv_sem, target).wait_send()

    def arrived(ref, sem):
        pltpu.make_async_copy(ref, ref, sem).wait()

    for which, ref in ((0, q_ref), (1, o_ref)):
        pltpu.make_async_copy(ref, raw.at[which], raw_got.at[which]).start()

    def stage_queries():
        for which in range(2):
            arrived(raw.at[which], raw_got.at[which])
            for u in range(srv):
                block = raw[which, :, :, pl.ds(u * HEAD_SIZE, HEAD_SIZE)].astype(jnp.float32)
                for j in range(pair):
                    stage[u, which, pl.ds(j * home, home), :] = block[:, j, :].astype(jnp.bfloat16)

    def by_row(source, target, u):
        heads_of = [source[u, pl.ds(j * home, home), :].astype(jnp.float32) for j in range(pair)]
        target[:, :, pl.ds(u * HEAD_SIZE, HEAD_SIZE)] = jnp.stack(heads_of, axis=1).astype(jnp.bfloat16)

    barrier = pltpu.get_barrier_semaphore()

    def greet(s, h, u):
        pl.semaphore_signal(barrier, inc=1, device_id=(s, h, u), device_id_type=MESH)

    for step in range(1, dp):
        greet((z + step) % dp, x, v)
    for step in range(1, heads):
        @pl.when(z > 0)
        def _():
            greet(z - 1, (x + step) % heads, v)

        @pl.when(z < dp - 1)
        def _():
            greet(z + 1, (x + step) % heads, v)
    for step in range(1, lanes):
        other = (lane + step) % lanes
        greet(z, other // srv, other % srv)
    sides = jnp.where(z > 0, 1, 0) + jnp.where(z < dp - 1, 1, 0)
    pl.semaphore_wait(barrier, lanes - 1 + sides * heads + dp - 1 - sides)

    def key_copies(act):
        def one(index, carry):
            side, h = index // heads, (x + index) % heads
            s = z + side - 1
            column = pl.ds(pl.multiple_of((h * srv + v) * HEAD_SIZE, HEAD_SIZE), HEAD_SIZE)
            start = first + home * s

            def each(at, count, slot):
                row = base + at - start

                @pl.when((s >= 0) & (s < dp) & (row >= 0) & (row < window))
                def _():
                    for which, ref in ((0, k_ref), (1, v_ref)):
                        act(
                            (s == z) & (h == x),
                            ref.at[pl.ds(pl.multiple_of(at, HALF), count), column],
                            kv_buf.at[row // TILE, which, pl.ds(pl.multiple_of(row % TILE, count), count), :],
                            kv_sem.at[index, slot, which],
                            kv_got.at[row // TILE],
                            (s, h, v),
                        )

            for c in range(rows // TILE):
                each(c * TILE + base % TILE, TILE, c)
            if rows % TILE:
                each(jnp.where(base % TILE == 0, rows - HALF, 0), HALF, rows // TILE)
            return carry

        lax.fori_loop(0, 3 * heads, one, 0)

    def doc_copies(act):
        for s in range(dp):
            act(z == s, doc_ref, docs.at[z], doc_sem.at[s], doc_got.at[z], (s, x, v))

    def query_copies(act):
        for u in range(srv):
            act(v == u, stage.at[u], qd_buf.at[:, v], q_sem.at[u], q_got.at[v], (z, x, u))

    key_copies(send)
    doc_copies(send)
    stage_queries()
    query_copies(send)

    top[...] = jnp.full_like(top, NEGATIVE / 10)
    norm[...] = jnp.zeros_like(norm)
    out_t[...] = jnp.zeros_like(out_t)
    dq_t[...] = jnp.zeros_like(dq_t)
    owned[...] = jnp.zeros_like(owned)

    def contract(a, b, left, right):
        return lax.dot_general(a, b, (((left,), (right,)), ((), ())), preferred_element_type=jnp.float32)

    def turned(a):
        return a.astype(jnp.float32).T.astype(jnp.bfloat16)

    for s in range(dp):
        arrived(docs.at[s], doc_got.at[s])
    home_tile = low_tile + tiles - 1
    query_doc = docs[home_tile // blocks, pl.ds(home_tile % blocks, 1), :]
    query_doc = jnp.broadcast_to(query_doc.astype(jnp.float32), (TILE, home))
    query_at = lax.broadcasted_iota(jnp.int32, (TILE, home), 1) + home_tile * TILE
    for u in range(srv):
        arrived(qd_buf.at[:, u], q_got.at[u])
        grad_t[:, pl.ds(u * wide, wide)] = qd_buf[1, u].astype(jnp.float32).T

    def relays(act, tile):
        shard = (low_tile + tile) // blocks

        @pl.when((shard > z) & (z > 0) & (tile < tiles - 1))
        def _():
            act(copy(kv_buf.at[tile], kv_buf.at[tile + 1], relay_sem.at[tile], kv_got.at[tile + 1], (z - 1, x, v)))

        @pl.when((shard < z) & (z < dp - 1) & (tile > 0))
        def _():
            act(copy(kv_buf.at[tile], kv_buf.at[tile - 1], relay_sem.at[tile], kv_got.at[tile - 1], (z + 1, x, v)))

    ahead = jnp.where((z > 0) & (z < dp - 1), AHEAD, 0)

    def forward(i, carry):
        def turn(i):
            return jnp.where(i < tiles - own_first, own_first + i, tiles - 1 - i)

        @pl.when(i < tiles)
        def _():
            tile = turn(i)
            arrived(kv_buf.at[tile], kv_got.at[tile])
            relays(lambda c: c.start(), tile)

        @pl.when((i >= ahead) & (i < tiles + ahead))
        def _():
            meet(turn(i - ahead))
        return carry

    def meet(tile):
        index = low_tile + tile
        key_doc = docs[index // blocks, pl.ds(index % blocks, 1), :]
        key_doc = jnp.broadcast_to(key_doc.astype(jnp.float32), (TILE, TILE)).T
        key_at = lax.broadcasted_iota(jnp.int32, (TILE, home), 0) + index * TILE
        bias = jnp.where((key_doc == query_doc) & (key_at <= query_at), 0.0, NEGATIVE)
        value_t = turned(kv_buf[tile, 1])
        keys = kv_buf[tile, 0]
        for u in range(srv):
            at = pl.ds(u * wide, wide)
            raw = contract(keys, qd_buf[0, u], 1, 1) + jnp.concatenate([bias] * pair, axis=1)
            scores[tile, :, at] = raw
            old = top[:, at]
            new = jnp.maximum(old, jnp.max(raw, axis=0, keepdims=True))
            weights = jnp.exp2((raw - new) * exponent)
            shrink = jnp.exp2((old - new) * exponent)
            top[:, at] = new
            norm[:, at] = norm[:, at] * shrink + jnp.sum(weights, axis=0, keepdims=True)
            out_t[:, at] = out_t[:, at] * shrink + contract(value_t, weights.astype(jnp.bfloat16), 1, 0)

    lax.fori_loop(0, tiles + AHEAD, forward, 0)

    def att_copy(act, u):
        act(v == u, att_out.at[u], att_in.at[v], att_sem.at[u], att_got.at[v], (z, x, u))

    def dq_copy(act, u):
        act(v == u, dq_out.at[u], dq_in.at[v], dq_sem.at[u], dq_got.at[v], (z, x, u))

    for u in range(srv):
        at = pl.ds(u * wide, wide)
        out = (out_t[:, at] / norm[:, at]).astype(jnp.bfloat16).astype(jnp.float32)
        out_t[:, at] = out
        delta[:, at] = jnp.sum(grad_t[:, at] * out, axis=0, keepdims=True)
        top[:, at] = top[:, at] * exponent + jnp.log2(norm[:, at])

    def part_copies(act, tile):
        shard = (low_tile + tile) // blocks

        @pl.when(shard > z)
        def _():
            act(copy(part.at[tile], up_in.at[tile], part_sem.at[tile], up_got.at[tile], (z + 1, x, v)))

        @pl.when(shard < z)
        def _():
            act(copy(part.at[tile], down_in.at[tile], part_sem.at[tile], down_got.at[tile], (z - 1, x, v)))

    def grad_copies(act, least, most):
        column = pl.ds(pl.multiple_of(lane * HEAD_SIZE, HEAD_SIZE), HEAD_SIZE)

        def one(j, carry):
            @pl.when((j * piece >= least) & (j * piece < most))
            def _():
                act(
                    lane == j,
                    owned.at[:, pl.ds(pl.multiple_of(j * piece, 16), piece), :],
                    g_ref.at[:, :, column],
                    g_sem.at[j],
                    g_got.at[lane],
                    (z, j // srv, j % srv),
                )
            return carry

        lax.fori_loop(0, lanes, one, 0)

    above_first = (low_tile // blocks == z + 1) & (low_tile % blocks > 0)

    def place(i):
        tile = jnp.where(i == 0, tiles - 1, jnp.where(i <= own_first, i - 1, tiles - 1 + own_first - i))
        return jnp.where(above_first & (i >= tiles - 2), 1 - tile, tile)

    extra = (z > 0) & ((low_tile - 1) // blocks == z)
    rest = jnp.minimum(jnp.maximum(low_tile - z * blocks, 0), blocks) * TILE
    idle = jnp.where(extra, jnp.maximum(rest - TILE - piece + 1, 0), rest)

    def waits_for(tile):
        shard = (low_tile + tile) // blocks
        above = (shard >= z) & (z > 0) & (tile < tiles - 1)
        below = (shard <= z) & (z < dp - 1) & (tile > 0)
        return above, below

    def finish(tile):
        index = low_tile + tile
        shard = index // blocks

        @pl.when(shard == z)
        def _():
            row = (index - z * blocks) * TILE
            owned[:, pl.ds(pl.multiple_of(row, TILE), TILE), :] = acc[tile].astype(jnp.bfloat16)
            grad_copies(send, jnp.where(extra & (row == rest), rest - piece + 1, row), row + TILE)

        @pl.when(shard != z)
        def _():
            part[tile] = acc[tile].astype(jnp.bfloat16)
        part_copies(lambda c: c.start(), tile)

    def compute(tile):
        key_t = turned(kv_buf[tile, 0])
        values = kv_buf[tile, 1]
        all_probs, all_grads = [], []
        for u in range(srv):
            at = pl.ds(u * wide, wide)
            probs = jnp.exp2(scores[tile, :, at] * exponent - top[:, at])
            weight_grad = contract(values, qd_buf[1, u], 1, 1)
            all_grads.append((probs * (weight_grad - delta[:, at])).astype(jnp.bfloat16))
            all_probs.append(probs.astype(jnp.bfloat16))
            dq_t[:, at] += contract(key_t, all_grads[-1], 1, 0)
        flat = (srv * wide, HEAD_SIZE)
        acc[tile, 0] = contract(jnp.concatenate(all_grads, axis=1), qd_buf[0].reshape(flat), 1, 0) * scale
        acc[tile, 1] = contract(jnp.concatenate(all_probs, axis=1), qd_buf[1].reshape(flat), 1, 0)

    def backward(i, carry):
        @pl.when(i < tiles)
        def _():
            tile = place(i)
            compute(tile)
            above, below = waits_for(tile)

            @pl.when(jnp.logical_not(above | below))
            def _():
                finish(tile)

        @pl.when((i >= 1) & (i <= srv))
        def _():
            u = i - 1
            att_out[u] = out_t[:, pl.ds(pl.multiple_of(u * wide, wide), wide)].T.astype(jnp.bfloat16)
            att_copy(send, u)

        @pl.when(i == tiles - 1)
        def _():
            for u in range(srv):
                dq_out[u] = (dq_t[:, pl.ds(u * wide, wide)] * scale).T.astype(jnp.bfloat16)
                dq_copy(send, u)

        @pl.when(i >= LAG)
        def _():
            tile = place(i - LAG)
            above, below = waits_for(tile)

            @pl.when(extra & (i - LAG == tiles - 1))
            def _():
                arrived(up_in.at[0], up_got.at[0])
                owned[:, pl.ds(pl.multiple_of(rest - TILE, TILE), TILE), :] = up_in[0]
                grad_copies(send, idle, rest - piece + 1)

            @pl.when(above)
            def _():
                arrived(up_in.at[tile + 1], up_got.at[tile + 1])
                acc[tile] += up_in[tile + 1].astype(jnp.float32)

            @pl.when(below)
            def _():
                arrived(down_in.at[tile - 1], down_got.at[tile - 1])
                acc[tile] += down_in[tile - 1].astype(jnp.float32)

            @pl.when(above | below)
            def _():
                finish(tile)
        return carry

    grad_copies(send, 0, idle)
    lax.fori_loop(0, tiles + LAG, backward, 0)


    for u in range(srv):
        arrived(att_in.at[u], att_got.at[u])
        by_row(att_in, att_ref, u)
    for u in range(srv):
        arrived(dq_in.at[u], dq_got.at[u])
        by_row(dq_in, dq_ref, u)
    doc_copies(sent)
    key_copies(sent)
    query_copies(sent)

    def settle(tile, carry):
        relays(lambda c: c.wait_send(), tile)
        part_copies(lambda c: c.wait_send(), tile)
        return carry

    lax.fori_loop(0, tiles, settle, 0)
    for u in range(srv):
        att_copy(sent, u)
        dq_copy(sent, u)
    grad_copies(sent, 0, blocks * TILE)
    for j in range(lanes):
        arrived(g_ref.at[:, :, pl.ds(j * HEAD_SIZE, HEAD_SIZE)], g_got.at[j])


def window_sizes(mesh_sizes, queries, keys):
    dp, heads, srv = mesh_sizes
    home, pair, width = queries.shape
    rows = keys.shape[0]
    key_total = rows * dp * heads
    longest = key_total // 2
    first = key_total - dp * home - longest
    return (dp, heads, srv, home, pair, rows, first, longest + home)


def window_fits(sizes, width):
    dp, heads, srv, home, pair, rows, first, window = sizes
    shard = rows * heads
    if width != srv * HEAD_SIZE or home != TILE or shard % TILE or first < 0 or first % TILE or window % TILE:
        return False
    if rows % HALF or rows % srv or (rows // srv) % 16 or rows % 16:
        return False
    blocks, tiles, start = shard // TILE, window // TILE, first // TILE
    for s in range(dp):
        held = set(range(start + s, start + s + tiles))
        for other in (s - 1, s + 1):
            if 0 <= other < dp:
                for tile in range(start + other, start + other + tiles):
                    beyond = tile // blocks > s if other < s else tile // blocks < s
                    owned = tile // blocks == s
                    if (beyond or owned) and tile not in held and not (owned and other < s and tile == start + other):
                        return False
                    through = tile // blocks > s if other < s else tile // blocks < s
                    if through and tile not in held:
                        return False
    return True


def local_window(sizes, queries, keys, values, output_gradient, doc_ids):
    dp, heads, srv, home, pair, rows, first, window = sizes
    width = queries.shape[2]
    wide = pair * home
    tiles = window // TILE
    piece = rows // srv
    chunks = -(-rows // TILE)

    docs = doc_ids.reshape(-1, TILE)
    vmem = pl.BlockSpec(memory_space=pltpu.VMEM)
    outside = pl.BlockSpec(memory_space=pltpu.HBM)
    sem = pltpu.SemaphoreType.DMA
    lanes = heads * srv
    b16, f32 = jnp.bfloat16, jnp.float32
    att, dq, kv = pl.pallas_call(
        functools.partial(attend, sizes),
        out_shape=(
            jax.ShapeDtypeStruct((home, pair, width), b16),
            jax.ShapeDtypeStruct((home, pair, width), b16),
            jax.ShapeDtypeStruct((2, piece, lanes * HEAD_SIZE), b16),
        ),
        in_specs=[outside] * 5,
        out_specs=(vmem, vmem, vmem),
        scratch_shapes=[
            pltpu.VMEM((2, home, pair, width), b16),
            pltpu.VMEM((srv, 2, wide, HEAD_SIZE), b16),
            pltpu.VMEM((2, srv, wide, HEAD_SIZE), b16),
            pltpu.VMEM((tiles, 2, TILE, HEAD_SIZE), b16),
            pltpu.VMEM((dp, docs.shape[0], TILE), jnp.int32),
            pltpu.VMEM((tiles, TILE, srv * wide), f32),
            pltpu.VMEM((1, srv * wide), f32),
            pltpu.VMEM((1, srv * wide), f32),
            pltpu.VMEM((1, srv * wide), f32),
            pltpu.VMEM((HEAD_SIZE, srv * wide), f32),
            pltpu.VMEM((HEAD_SIZE, srv * wide), f32),
            pltpu.VMEM((HEAD_SIZE, srv * wide), f32),
            pltpu.VMEM((tiles, 2, TILE, HEAD_SIZE), f32),
            pltpu.VMEM((tiles, 2, TILE, HEAD_SIZE), b16),
            pltpu.VMEM((tiles, 2, TILE, HEAD_SIZE), b16),
            pltpu.VMEM((tiles, 2, TILE, HEAD_SIZE), b16),
            pltpu.VMEM((2, rows * heads, HEAD_SIZE), b16),
            pltpu.VMEM((srv, wide, HEAD_SIZE), b16),
            pltpu.VMEM((srv, wide, HEAD_SIZE), b16),
            pltpu.VMEM((srv, wide, HEAD_SIZE), b16),
            pltpu.VMEM((srv, wide, HEAD_SIZE), b16),
            sem((2,)), sem((srv,)), sem((srv,)),
            sem((3 * heads, chunks, 2)), sem((tiles,)), sem((tiles,)),
            sem((dp,)), sem((dp,)),
            sem((srv,)), sem((srv,)),
            sem((srv,)), sem((srv,)),
            sem((tiles,)), sem((tiles,)), sem((tiles,)),
            sem((lanes,)), sem((lanes,)),
        ],
        compiler_params=pltpu.CompilerParams(
            collective_id=0, has_side_effects=True, vmem_limit_bytes=63 * 1024 * 1024
        ),
    )(queries, output_gradient, keys, values, docs)

    return att, dq, kv[0], kv[1]


def local_spread(queries, keys, values, output_gradient, doc_ids):
    home_rows, pair_heads, group_width = queries.shape
    groups = group_width // HEAD_SIZE
    scale_factor = HEAD_SIZE ** (-0.5)
    key_rows, value_rows = (
        lax.all_to_all(keys, "head", split_axis=1, concat_axis=0, tiled=True),
        lax.all_to_all(values, "head", split_axis=1, concat_axis=0, tiled=True),
    )
    key_count = key_rows.shape[0]
    servers = lax.axis_size("dp")
    server = lax.axis_index("dp")
    key_at = server * key_count + jnp.arange(key_count, dtype=jnp.int32)
    all_docs = lax.all_gather(doc_ids, "dp", axis=0, tiled=True)
    query_total = home_rows * servers
    context = all_docs.shape[0] - query_total
    query_docs = all_docs[context:]
    query_places = context + jnp.arange(query_total, dtype=jnp.int32)
    all_q, all_dout = (
        lax.all_gather(queries, "dp", axis=0, tiled=True),
        lax.all_gather(output_gradient, "dp", axis=0, tiled=True),
    )
    block_rows = math.gcd(512, query_total)
    block_count = query_total // block_rows
    key_heads = key_rows.reshape(key_count, groups, HEAD_SIZE)
    value_heads = value_rows.reshape(key_count, groups, HEAD_SIZE)
    query_blocks = all_q.reshape(block_count, block_rows, pair_heads, groups, HEAD_SIZE)
    grad_blocks = all_dout.reshape(block_count, block_rows, pair_heads, groups, HEAD_SIZE)
    place_blocks = query_places.reshape(block_count, block_rows)
    doc_blocks = query_docs.reshape(block_count, block_rows)

    def admissible(places, query_doc):
        return (key_at[None, :] <= places[:, None]) & (doc_ids[None, :] == query_doc[:, None])

    def scores_of(query_block):
        return (
            jnp.einsum("pjgd,kgd->gjpk", query_block, key_heads, preferred_element_type=jnp.float32)
            * scale_factor
        )

    def block_max(inputs):
        query_block, places, query_doc = inputs
        allowed = admissible(places, query_doc)

        def compute():
            raw_scores = scores_of(query_block)
            masked = jnp.where(allowed[None, None], raw_scores, NEGATIVE)
            return (jnp.max(masked, axis=-1).transpose(2, 1, 0), raw_scores)

        return compute()

    def block_top(inputs):
        return block_max(inputs)[0]

    local_max = lax.map(block_top, (query_blocks, place_blocks, doc_blocks))
    row_max = lax.pmax(local_max.reshape(query_total, pair_heads, groups), "dp")
    max_blocks = row_max.reshape(block_count, block_rows, pair_heads, groups)

    def block_sum(inputs):
        stored, places, query_doc, row_top = inputs
        allowed = admissible(places, query_doc)

        def compute():
            block_scores = scores_of(stored)
            shifted = block_scores - row_top.transpose(2, 1, 0)[..., None]
            weights = jnp.where(allowed[None, None], jnp.exp(shifted), 0.0)
            weighted = jnp.einsum(
                "gjpk,kgd->pjgd",
                weights.astype(jnp.bfloat16),
                value_heads,
                preferred_element_type=jnp.float32,
            )
            return (
                weighted.reshape(block_rows, pair_heads, group_width),
                jnp.sum(weights, axis=-1).transpose(2, 1, 0),
            )

        return compute()

    part_out, part_norm = lax.map(block_sum, (query_blocks, place_blocks, doc_blocks, max_blocks))
    part_out = part_out.reshape(query_total, pair_heads, group_width)
    part_norm = part_norm.reshape(query_total, pair_heads, groups)
    home_out, home_norm = (
        lax.psum_scatter(part_out, "dp", scatter_dimension=0, tiled=True),
        lax.psum_scatter(part_norm, "dp", scatter_dimension=0, tiled=True),
    )
    home_max = lax.dynamic_slice_in_dim(row_max, server * home_rows, home_rows, 0)
    attn_home = (
        home_out.reshape(home_rows, pair_heads, groups, HEAD_SIZE) / home_norm[..., None]
    ).astype(jnp.bfloat16)
    log_home = home_max + jnp.log(home_norm)
    grad_home = output_gradient.reshape(home_rows, pair_heads, groups, HEAD_SIZE).astype(
        jnp.float32
    )
    delta_home = jnp.sum(grad_home * attn_home.astype(jnp.float32), axis=-1)
    log_all, delta_all = (
        lax.all_gather(log_home, "dp", axis=0, tiled=True),
        lax.all_gather(delta_home, "dp", axis=0, tiled=True),
    )
    attention = attn_home.reshape(home_rows, pair_heads, group_width)
    log_blocks = log_all.reshape(block_count, block_rows, pair_heads, groups)
    delta_blocks = delta_all.reshape(block_count, block_rows, pair_heads, groups)

    def block_grad(totals, inputs):
        query_block, grad_block, places, query_doc, log_norm, row_delta = inputs
        allowed = admissible(places, query_doc)

        def compute():
            shifted = scores_of(query_block) - log_norm.transpose(2, 1, 0)[..., None]
            probs = jnp.where(allowed[None, None], jnp.exp(shifted), 0.0)
            value_grad = jnp.einsum(
                "gjpk,pjgd->kgd",
                probs.astype(jnp.bfloat16),
                grad_block,
                preferred_element_type=jnp.float32,
            )
            weight_grad = jnp.einsum(
                "pjgd,kgd->gjpk", grad_block, value_heads, preferred_element_type=jnp.float32
            )
            score_grad = (probs * (weight_grad - row_delta.transpose(2, 1, 0)[..., None])).astype(
                jnp.bfloat16
            )
            query_grad = (
                jnp.einsum(
                    "gjpk,kgd->pjgd", score_grad, key_heads, preferred_element_type=jnp.float32
                )
                * scale_factor
            )
            key_grad = (
                jnp.einsum(
                    "gjpk,pjgd->kgd", score_grad, query_block, preferred_element_type=jnp.float32
                )
                * scale_factor
            )
            return (query_grad.reshape(block_rows, pair_heads, group_width), key_grad, value_grad)

        query_grad, key_grad, value_grad = compute()
        return ((totals[0] + key_grad, totals[1] + value_grad), query_grad)

    zero_start = jnp.zeros((key_count, groups, HEAD_SIZE), jnp.float32)
    grad_inputs = (query_blocks, grad_blocks, place_blocks, doc_blocks, log_blocks, delta_blocks)
    (key_total, value_total), query_parts = lax.scan(
        block_grad, (zero_start, zero_start), grad_inputs
    )
    q_summed = lax.psum_scatter(
        query_parts.reshape(query_total, pair_heads, group_width).astype(jnp.bfloat16),
        "dp",
        scatter_dimension=0,
        tiled=True,
    )
    spread_key, spread_value = (
        lax.all_to_all(
            key_total.reshape(key_count, group_width).astype(jnp.bfloat16),
            "head",
            split_axis=0,
            concat_axis=1,
            tiled=True,
        ).astype(jnp.float32),
        lax.all_to_all(
            value_total.reshape(key_count, group_width).astype(jnp.bfloat16),
            "head",
            split_axis=0,
            concat_axis=1,
            tiled=True,
        ).astype(jnp.float32),
    )
    k_summed, v_summed = (
        lax.psum_scatter(
            spread_key.astype(jnp.bfloat16), "srv", scatter_dimension=0, tiled=True
        ).astype(jnp.float32),
        lax.psum_scatter(
            spread_value.astype(jnp.bfloat16), "srv", scatter_dimension=0, tiled=True
        ).astype(jnp.float32),
    )
    return (attention, q_summed, k_summed.astype(jnp.bfloat16), v_summed.astype(jnp.bfloat16))


def solution(mesh):
    placed = (
        P("dp", "srv", "head"),
        P(("dp", "head"), None),
        P(("dp", "head"), None),
        P("dp", "srv", "head"),
        P("dp"),
    )
    mesh_sizes = tuple(mesh.shape[name] for name in AXES)

    def local(queries, keys, values, output_gradient, doc_ids):
        args = (queries, keys, values, output_gradient, doc_ids)
        sizes = window_sizes(mesh_sizes, queries, keys)
        if window_fits(sizes, queries.shape[2]):
            return local_window(sizes, *args)
        return local_spread(*args)

    return jax.shard_map(
        local,
        mesh=mesh,
        in_specs=placed,
        out_specs=(
            P("dp", "srv", "head"),
            P("dp", "srv", "head"),
            P(("dp", "head", "srv"), None),
            P(("dp", "head", "srv"), None),
        ),
        check_vma=False,
    )
```
